512 devices in a mesh: row: 16 (over x, z_lo), col: 32 (over y, z_hi, core).
Axes of the slice: x: 4, y: 4, z: 16 (z_hi: 4, z_lo: 4; z = z_hi * 4 + z_lo), core: 2. Of those that a mesh axis runs over, the one named last changes fastest.
Arguments:
- layer_input: bfloat16 [2560, 8192], P('col', 'row'), may hold values from -6 to 6
- w_query: bfloat16 [8192, 8192], P('row', 'col'), may hold values from -0.0625 to 0.0625
- w_key: bfloat16 [8192, 1024], P('row', 'col'), may hold values from -0.0625 to 0.0625
- w_value: bfloat16 [8192, 1024], P('row', 'col'), may hold values from -0.0625 to 0.0625
- rotated_query_state: bfloat16 [2560, 8192], P('row', 'col'), may hold values from -156 to 156
- rotated_key_state: bfloat16 [2560, 1024], P('row', 'col'), may hold values from -6 to 6
- saved_value_state: bfloat16 [2560, 1024], P('row', 'col'), may hold values from -6 to 6
- context_gradient: bfloat16 [2560, 8192], P('row', 'col'), may hold values from -24 to 24
- positions: int32 [2560], P('row'), may hold values from 0 to 1982, as said below
- segment_ids: int32 [2560], P('row'), may hold values from 0 to 1, as said below
Outputs:
- grad_input: bfloat16 [2560, 8192], P('col', 'row')
- grad_wq: float32 [8192, 8192], P('row', 'col')
- grad_wk: float32 [8192, 1024], P('row', 'col')
- grad_wv: float32 [8192, 1024], P('row', 'col')
The draws below stay inside these ranges and needn't reach their ends.
Inputs may be any that keep to these rules, and one draw needn't show every extreme that they name: `segment_ids`: never falls along the tokens; each of the 2 rollouts holds at least one token. `positions`: rises by one from each token to the next within a rollout.
All inputs are finite; a program needn't handle non-finite values.
Results may differ from the reference program's by a relative error of at most 0.025.
Values may be sent and summed in bfloat16 or wider, within the bound.
A program may use at most 64 MiB of HBM per device.

```python
import math
import jax
import jax.numpy as jnp
from jax import lax

D = 8192
QUERY_HEADS = 64
KEY_VALUE_HEADS = 8
HEAD_SIZE = 128
TOK_DEV = 160
ROLLOUTS = 2
BATCH_TOKENS = 2560
QUERY_FEATURES = 8192
KD = 1024
N_ROW = 16
N_COL = 32


def rollout_layout(key):
    jitter_reach = BATCH_TOKENS // (4 * ROLLOUTS)
    jitter = jax.random.randint(jax.random.fold_in(key, 11), (ROLLOUTS - 1,), -jitter_reach, jitter_reach + 1)
    cut_points = (jnp.arange(1, ROLLOUTS, dtype=jnp.int32) * (BATCH_TOKENS // ROLLOUTS) + jitter).astype(jnp.int32)
    token_index = jnp.arange(BATCH_TOKENS, dtype=jnp.int32)
    rollout_ids = jnp.sum((token_index[:, None] >= cut_points[None, :]).astype(jnp.int32), axis=1)
    starts = jnp.concatenate([jnp.zeros((1,), jnp.int32), cut_points])
    random_shift = jax.random.randint(jax.random.fold_in(key, 12), (ROLLOUTS,), 0, 64).astype(jnp.int32)
    top_position = BATCH_TOKENS // ROLLOUTS + 2 * jitter_reach + 62
    first_shift = (top_position + 1 - cut_points[0]).astype(jnp.int32)
    rollout_index = jnp.arange(ROLLOUTS, dtype=jnp.int32)
    prompt_shift = jnp.where(rollout_index == 0, first_shift, jnp.where(rollout_index == ROLLOUTS - 1, 0, random_shift)).astype(jnp.int32)
    onehot = (rollout_ids[:, None] == rollout_index[None, :]).astype(jnp.int32)
    begin_index = jnp.sum(onehot * starts[None, :], axis=1)
    shift_here = jnp.sum(onehot * prompt_shift[None, :], axis=1)
    return (rollout_ids.astype(jnp.int32), (token_index - begin_index + shift_here).astype(jnp.int32))


def drawn_pair(key, strength):
    base_query = jnp.clip(jax.random.normal(jax.random.fold_in(key, 21), (BATCH_TOKENS, QUERY_FEATURES), jnp.float32), -6.0, 6.0)
    base_key = jnp.clip(jax.random.normal(jax.random.fold_in(key, 22), (BATCH_TOKENS, KD), jnp.float32), -6.0, 6.0)
    token_index = jnp.arange(BATCH_TOKENS)
    anchor = (token_index % 61 == 30).astype(jnp.float32) * strength
    before = jnp.roll(anchor, -1)
    follow = jnp.roll(base_key, -1, axis=0)
    key_token_rows = base_key * (1.0 - before[:, None]) + 0.99 * follow * before[:, None]
    query_rows = base_query * (1.0 - anchor[:, None])
    return (query_rows, key_token_rows)


def draw_segment_ids(key, part):
    rollout_ids, position_rows = rollout_layout(key)
    return rollout_ids


def draw_positions(key, part):
    rollout_ids, position_rows = rollout_layout(key)
    return position_rows


def draw_rotated_query_state(key, part):
    query_rows, key_token_rows = drawn_pair(key, 0.0)
    return query_rows.astype(jnp.bfloat16)


def draw_rotated_key_state(key, part):
    query_rows, key_token_rows = drawn_pair(key, 0.0)
    return key_token_rows.astype(jnp.bfloat16)


def steps_of(key, dims, cuts, low, largest):
    loudness, own = 1.0, jax.random.fold_in(key, 6)
    for axis_at, blocks in cuts:
        steps = jnp.exp(jax.random.uniform(jax.random.fold_in(own, axis_at), (blocks,), jnp.float32, low / len(cuts), largest / len(cuts)))
        loudness = loudness * jnp.repeat(steps, dims[axis_at] // blocks).reshape([-1 if axis == axis_at else 1 for axis in range(len(dims))])
    return loudness


def noise(key, shape, deviation, bound, split=(), kind=jnp.bfloat16):
    drawn = deviation * jax.random.normal(key, shape, jnp.float32)
    if split:
        drawn = drawn * steps_of(key, shape, split, -0.22, 0.18)
    return jnp.clip(drawn, -bound, bound).astype(kind)


def setup_inputs(seed: int = 0) -> dict:
    splits = jax.random.split(jax.random.key(seed), 11)
    layer_input = noise(splits[0], (BATCH_TOKENS, D), 1.0, 6.0, ((0, 32), (1, 16)))
    w_query = noise(splits[1], (D, QUERY_FEATURES), D ** -0.5, 0.0625, ((0, 16), (1, 32)))
    w_key = noise(splits[2], (D, KD), D ** -0.5, 0.0625, ((0, 16), (1, 32)))
    w_value = noise(splits[3], (D, KD), D ** -0.5, 0.0625, ((0, 16), (1, 32)))
    rotated_query_state = draw_rotated_query_state(jax.random.fold_in(splits[10], 71), 0)
    rotated_key_state = draw_rotated_key_state(jax.random.fold_in(splits[10], 71), 0)
    saved_value_state = noise(splits[6], (BATCH_TOKENS, KD), 1.0, 6.0, ((0, 16), (1, 32)))
    context_gradient = noise(splits[7], (BATCH_TOKENS, QUERY_FEATURES), 4.0, 24.0, ((0, 16), (1, 32)))
    positions = draw_positions(jax.random.fold_in(splits[10], 71), 0)
    segment_ids = draw_segment_ids(jax.random.fold_in(splits[10], 71), 0)
    return dict(layer_input=layer_input, w_query=w_query, w_key=w_key, w_value=w_value, rotated_query_state=rotated_query_state, rotated_key_state=rotated_key_state, saved_value_state=saved_value_state, context_gradient=context_gradient, positions=positions, segment_ids=segment_ids)


rope_base = 500000.0


def contract(left, right, left_dim, right_dim):
    return lax.dot_general(left, right, (((left_dim,), (right_dim,)), ((), ())), preferred_element_type=jnp.float32)


def rope_tables(positions):
    half_width = HEAD_SIZE // 2
    freq = jnp.exp(-(2.0 * jnp.arange(half_width, dtype=jnp.float32) / HEAD_SIZE) * math.log(rope_base))
    angle = positions.astype(jnp.float32)[:, None] * freq[None, :]
    return jnp.cos(angle), jnp.sin(angle)


def unrotate(gradient, cosine, sine):
    half_width = gradient.shape[-1] // 2
    first = gradient[..., :half_width]
    second = gradient[..., half_width:]
    return jnp.concatenate([first * cosine + second * sine, second * cosine - first * sine], axis=-1)


def blocked_partials(left, right, shared_heads, per_share):
    left_blocks = left.astype(jnp.float32).reshape(shared_heads, per_share, N_ROW, TOK_DEV, BATCH_TOKENS)
    right_blocks = right.astype(jnp.float32).reshape(shared_heads, per_share, N_ROW, TOK_DEV, HEAD_SIZE)
    parts = jnp.einsum("jhbts,jhbtd->jbsd", left_blocks, right_blocks)
    rounded = lax.optimization_barrier(parts.astype(jnp.bfloat16)).astype(jnp.float32)
    return jnp.sum(rounded, axis=(0, 1))


def reference(layer_input, w_query, w_key, w_value, rotated_query_state, rotated_key_state, saved_value_state, context_gradient, positions, segment_ids):
    score_scale = HEAD_SIZE ** -0.5
    heads_per_group = QUERY_HEADS // KEY_VALUE_HEADS
    shared_heads = N_COL // KEY_VALUE_HEADS
    per_share = heads_per_group // shared_heads
    visible = (segment_ids[:, None] == segment_ids[None, :]) & (positions[None, :] <= positions[:, None])
    query_grouped = rotated_query_state.reshape(BATCH_TOKENS, KEY_VALUE_HEADS, heads_per_group * HEAD_SIZE).transpose(1, 0, 2)
    gradient_grouped = context_gradient.reshape(BATCH_TOKENS, KEY_VALUE_HEADS, heads_per_group * HEAD_SIZE).transpose(1, 0, 2)
    key_grouped = rotated_key_state.reshape(BATCH_TOKENS, KEY_VALUE_HEADS, HEAD_SIZE).transpose(1, 0, 2)
    value_grouped = saved_value_state.reshape(BATCH_TOKENS, KEY_VALUE_HEADS, HEAD_SIZE).transpose(1, 0, 2)

    def one_group(operands):
        query_part, grad_part, key_part, value_part = operands
        query_rows = query_part.reshape(BATCH_TOKENS, heads_per_group, HEAD_SIZE).transpose(1, 0, 2).reshape(heads_per_group * BATCH_TOKENS, HEAD_SIZE)
        grad_rows = grad_part.reshape(BATCH_TOKENS, heads_per_group, HEAD_SIZE).transpose(1, 0, 2).reshape(heads_per_group * BATCH_TOKENS, HEAD_SIZE)
        scores = (contract(query_rows, key_part, 1, 1) * score_scale).reshape(heads_per_group, BATCH_TOKENS, BATCH_TOKENS)
        row_peak = jnp.max(jnp.where(visible[None], scores, -1e30), axis=-1, keepdims=True)
        exponent_terms = jnp.where(visible[None], jnp.exp(scores - row_peak), 0.0)
        weights = exponent_terms / jnp.sum(exponent_terms, axis=-1, keepdims=True)
        weights_low = weights.astype(jnp.bfloat16)
        dweights = contract(grad_rows, value_part, 1, 1).reshape(heads_per_group, BATCH_TOKENS, BATCH_TOKENS)
        row_delta = jnp.sum(weights * dweights, axis=-1, keepdims=True)
        dscores = (weights * (dweights - row_delta) * score_scale).astype(jnp.bfloat16)
        flat_dscores = dscores.reshape(heads_per_group * BATCH_TOKENS, BATCH_TOKENS)
        dquery_rot = contract(flat_dscores, key_part, 1, 0).reshape(heads_per_group, BATCH_TOKENS, HEAD_SIZE).transpose(1, 0, 2)
        dkey_rot = blocked_partials(dscores, query_rows, shared_heads, per_share)
        dvalue = blocked_partials(weights_low, grad_rows, shared_heads, per_share)
        return dquery_rot, dkey_rot, dvalue

    dquery_rot, dkey_rot, dvalue = lax.map(one_group, (query_grouped, gradient_grouped, key_grouped, value_grouped))
    dquery_rot = dquery_rot.transpose(1, 0, 2, 3).reshape(BATCH_TOKENS, QUERY_HEADS, HEAD_SIZE)
    dkey_rot = dkey_rot.transpose(1, 0, 2)
    cosine, sine = rope_tables(positions)
    dquery = unrotate(dquery_rot, cosine[:, None], sine[:, None]).reshape(BATCH_TOKENS, QUERY_FEATURES).astype(jnp.bfloat16)
    dkey = unrotate(dkey_rot, cosine[:, None], sine[:, None]).reshape(BATCH_TOKENS, KD).astype(jnp.bfloat16)
    dvalue_low = dvalue.transpose(1, 0, 2).reshape(BATCH_TOKENS, KD).astype(jnp.bfloat16)
    grad_wq = contract(layer_input, dquery, 0, 0)
    grad_wk = contract(layer_input, dkey, 0, 0)
    grad_wv = contract(layer_input, dvalue_low, 0, 0)
    query_cols = QUERY_FEATURES // N_COL
    key_cols = KD // N_COL
    grad_blocks = jnp.concatenate([dquery.reshape(BATCH_TOKENS, N_COL, query_cols), dkey.reshape(BATCH_TOKENS, N_COL, key_cols), dvalue_low.reshape(BATCH_TOKENS, N_COL, key_cols)], axis=2).transpose(1, 0, 2)
    weight_blocks = jnp.concatenate([w_query.reshape(D, N_COL, query_cols), w_key.reshape(D, N_COL, key_cols), w_value.reshape(D, N_COL, key_cols)], axis=2).transpose(1, 0, 2)

    def accumulate(running, operands):
        grad_block, weight_block = operands
        partial_sum = contract(grad_block, weight_block, 1, 1)
        rounded = lax.optimization_barrier(partial_sum.astype(jnp.bfloat16)).astype(jnp.float32)
        return running + rounded, None

    summed, unused_out = lax.scan(accumulate, jnp.zeros((BATCH_TOKENS, D), jnp.float32), (grad_blocks, weight_blocks))
    return summed.astype(jnp.bfloat16), grad_wq, grad_wk, grad_wv
```

```python
import math

import jax
import jax.numpy as jnp
from jax import lax
from jax.experimental import pallas as pl
from jax.experimental.pallas import tpu as pltpu
from jax.sharding import PartitionSpec as P

MESH = pl.DeviceIdType.MESH
BF = jnp.bfloat16
F32 = jnp.float32
HEAD = 128
TOK = 160
HALF = 80
LANES = 384
ROPE_BASE = 500000.0
SCALE = HEAD ** (-0.5)


def dot(a, b):
    return lax.dot_general(a, b, (((1,), (0,)), ((), ())), preferred_element_type=F32)


def dot_first(a, b):
    return lax.dot_general(a, b, (((0,), (0,)), ((), ())), preferred_element_type=F32)


def unrotate(first, second, cosine, sine):
    return first * cosine + second * sine, second * cosine - first * sine


def kernel(
    x_ref, wq_ref, wk_ref, wv_ref, q_ref, k_ref, v_ref, o_ref, seg_ref, cos_ref, sin_ref,
    gi_ref, gwq_ref, gwk_ref, gwv_ref,
    kv, kf, vf, sc, dw, qt, ot, qr, orow, wqt, wqtp, wkv, wkvp, wka, wkb, dqacc,
    dkp, dkr, t1, xr, t2, zr, cb, pg, pgp, dqg, dqp, xg, gi, gyr, gys, gzr, accq, acck,
    kz_s, kz_r, kx_s, kx_r, kc_s, kc_r, w_s, w_r,
    xz_s, xz_r, xy_s, xy_r, xc_s, xc_r,
    dc_s, dc_r, dx_s, dx_r, dz_s, dz_r, cx_s, cx_r, pz_s, pz_r, px_s, px_r, pc_s, pc_r,
    qz_s, qz_r, qx_s, qx_r, qc_s, qc_r, gy_s, gy_r, gz_s, gz_r,
):
    row, col = lax.axis_index("row"), lax.axis_index("col")
    x, zl = lax.div(row, 4), lax.rem(row, 4)
    y, zh, k = lax.div(col, 8), lax.rem(lax.div(col, 2), 4), lax.rem(col, 2)
    pair, h = lax.div(zh, 2), lax.rem(zh, 2)
    w = h * 4 + zl

    def device(x_=x, zl_=zl, y_=y, zh_=zh, k_=k):
        return (x_ * 4 + zl_, y_ * 8 + zh_ * 2 + k_)

    def at_x(d):
        return device(x_=lax.rem(x + d, 4))

    def at_y(d):
        return device(y_=lax.rem(y + d, 4))

    def at_zh(d):
        return device(zh_=lax.rem(zh + d, 4))

    def at_zl(d):
        return device(zl_=lax.rem(zl + d, 4))

    def at_run(e):
        there = lax.rem(w + e, 8)
        return device(zl_=lax.rem(there, 4), zh_=pair * 2 + lax.div(there, 4))

    mate = device(k_=1 - k)
    across = device(zh_=pair * 2 + 1 - h)
    diagonal = device(zh_=pair * 2 + 1 - h, k_=1 - k)
    far = [device(zh_=(1 - pair) * 2 + i) for i in range(2)]

    pending = []

    def send(src, dst, s_sem, r_sem, to):
        copy = pltpu.make_async_remote_copy(
            src_ref=src, dst_ref=dst, send_sem=s_sem, recv_sem=r_sem,
            device_id=to, device_id_type=MESH,
        )
        copy.start()
        pending.append(copy)

    def receive(dst, r_sem, s_sem):
        pltpu.make_async_remote_copy(
            src_ref=dst, dst_ref=dst, send_sem=s_sem, recv_sem=r_sem,
            device_id=mate, device_id_type=MESH,
        ).wait_recv()

    barrier = pltpu.get_barrier_semaphore()
    peers = [mate, diagonal] + far
    peers += [at_x(d) for d in (1, 2, 3)] + [at_y(d) for d in (1, 2, 3)]
    peers += [at_run(e) for e in range(1, 8)]
    for peer in peers:
        pl.semaphore_signal(barrier, inc=1, device_id=peer, device_id_type=MESH)

    keys, values = k_ref[...], v_ref[...]
    kv[k, x, w, 0:HALF, :] = jnp.concatenate(
        [keys[:HALF], values[:HALF], keys[HALF:], values[HALF:]], axis=1
    )
    first_count = jnp.sum(jnp.where(seg_ref[...] == 0, 1.0, 0.0), axis=1, keepdims=True)
    kv[k, x, w, HALF:96, :] = jnp.broadcast_to(first_count, (16, 128)).astype(BF)

    pl.semaphore_wait(barrier, len(peers))

    for e in range(1, 8):
        block = kv.at[k, x, w]
        send(block, block, kz_s.at[e], kz_r.at[e], at_run(e))

    xg[y, zh, k] = x_ref[...]
    qr[0:TOK] = q_ref[:, 0:128]
    qr[TOK : 2 * TOK] = q_ref[:, 128:256]
    qr[2 * TOK : LANES] = jnp.zeros((LANES - 2 * TOK, 128), BF)
    orow[0:TOK] = o_ref[:, 0:128]
    orow[TOK : 2 * TOK] = o_ref[:, 128:256]
    orow[2 * TOK : LANES] = jnp.zeros((LANES - 2 * TOK, 128), BF)
    qt[...] = qr[...].astype(F32).T.astype(BF)
    ot[...] = orow[...].astype(F32).T.astype(BF)
    wqt[...] = wq_ref[...].astype(F32).T.astype(BF)
    kv_weights = jnp.concatenate([wk_ref[...], wv_ref[...]], axis=1)
    wkv[...] = jnp.concatenate([kv_weights, kv_weights], axis=1).astype(F32).T.astype(BF)
    send(wqt, wqtp, w_s.at[0], w_r.at[0], mate)
    send(wkv, wkvp, w_s.at[1], w_r.at[1], mate)

    for e in range(1, 8):
        block = kv.at[k, x, lax.rem(w + 8 - e, 8)]
        receive(block, kz_r.at[e], kz_s.at[e])
    for d in (1, 3, 2):
        send(kv.at[k, x], kv.at[k, x], kx_s.at[d], kx_r.at[d], at_x(d))
    send(kv.at[k, x], kv.at[k, x], kc_s.at[0], kc_r.at[0], mate)
    for d in (1, 3, 2):
        block = xg.at[y, zh, k]
        send(block, block, xz_s.at[d], xz_r.at[d], at_zh(d))

    def products(there):
        def step(i, _):
            at = there * 4 + i
            for half in range(2):
                parts = [kv[kk, there, hh * 4 + i, 0:HALF, :] for hh in range(2) for kk in range(2)]
                lo = 64 * half
                kf[at, half * HALF : (half + 1) * HALF, :] = jnp.concatenate(
                    [p[:, lo : lo + 32] for p in parts], axis=1
                )
                vf[at, half * HALF : (half + 1) * HALF, :] = jnp.concatenate(
                    [p[:, lo + 32 : lo + 64] for p in parts], axis=1
                )
            sc[at] = dot(kf[at], qt[...]) * SCALE
            dw[at] = dot(vf[at], ot[...])
            return 0

        lax.fori_loop(0, 4, step, 0)

    receive(kv.at[1 - k, x], kc_r.at[0], kc_s.at[0])
    products(x)
    for d in (1, 3, 2):
        there = lax.rem(x + 4 - d, 4)
        receive(kv.at[k, there], kx_r.at[d], kx_s.at[d])
        send(kv.at[k, there], kv.at[k, there], kc_s.at[d], kc_r.at[d], mate)
    for d in (1, 3, 2):
        there = lax.rem(x + 4 - d, 4)
        receive(kv.at[1 - k, there], kc_r.at[d], kc_s.at[d])
        products(there)

    for d in (1, 3, 2):
        receive(xg.at[y, lax.rem(zh + 4 - d, 4), k], xz_r.at[d], xz_s.at[d])
    for d in (1, 3, 2):
        block = xg.at[y, :, k]
        send(block, block, xy_s.at[d], xy_r.at[d], at_y(d))
    block = xg.at[y, :, k]
    send(block, block, xc_s.at[0], xc_r.at[0], mate)

    cut = jnp.zeros((1, 1), F32)
    for xx in range(4):
        for zz in range(4):
            cut = cut + kv[k, xx, zz, HALF : HALF + 16, :].astype(F32)[0:1, 0:1]
    lane = lax.broadcasted_iota(jnp.int32, (1, LANES), 1)
    query = lane - TOK * (lane >= TOK).astype(jnp.int32) - TOK * (lane >= 2 * TOK).astype(jnp.int32)
    query = query + row * TOK
    cut = jnp.broadcast_to(cut, (1, LANES)).astype(jnp.int32)
    begin = jnp.where(query < cut, 0, cut)

    def mask_step(b, peak):
        key = b * TOK + lax.broadcasted_iota(jnp.int32, (TOK, LANES), 0)
        seen = jnp.where((key >= begin) & (key <= query), sc[b], -1e30)
        sc[b] = seen
        return jnp.maximum(peak, jnp.max(seen, axis=0, keepdims=True))

    peak = lax.fori_loop(0, 16, mask_step, jnp.full((1, LANES), -1e30, F32))

    def sum_step(b, sums):
        total, delta = sums
        term = jnp.exp(sc[b] - peak)
        sc[b] = term
        return (
            total + jnp.sum(term, axis=0, keepdims=True),
            delta + jnp.sum(term * dw[b], axis=0, keepdims=True),
        )

    zero = jnp.zeros((1, LANES), F32)
    total, delta = lax.fori_loop(0, 16, sum_step, (zero, zero))
    inverse = 1.0 / total
    delta = delta * inverse

    dqacc[...] = jnp.zeros_like(dqacc)
    for d in range(4):
        there = lax.rem(x + d, 4)

        def grad_step(i, _):
            b = there * 4 + i
            weights = sc[b] * inverse
            dscores = (weights * (dw[b] - delta) * SCALE).astype(BF)
            dkey = dot(dscores, qr[...]).astype(BF)
            dvalue = dot(weights.astype(BF), orow[...]).astype(BF)
            dqacc[...] += dot_first(kf[b], dscores)
            for half in range(2):
                dkp[half, there, i, 0] = dkey[half * HALF : (half + 1) * HALF]
                dkp[half, there, i, 1] = dvalue[half * HALF : (half + 1) * HALF]
            return 0

        lax.fori_loop(0, 4, grad_step, 0)
        send(dkp.at[1 - k, there], dkr.at[there], dc_s.at[d], dc_r.at[d], mate)

    cosine, sine = cos_ref[...], sin_ref[...]
    dquery = dqacc[...].T
    for head in range(2):
        part = dquery[head * TOK : (head + 1) * TOK]
        first, second = unrotate(part[:, :64], part[:, 64:], cosine, sine)
        both = jnp.concatenate([first, second], axis=1).astype(BF)
        for half in range(2):
            dqg[x, zl, half, :, head * 128 : (head + 1) * 128] = both[half * HALF : (half + 1) * HALF]
    for d in (1, 3, 2):
        block = dqg.at[x, zl]
        send(block, block, qz_s.at[d], qz_r.at[d], at_zl(d))

    for d in (1, 3, 2, 0):
        there = lax.rem(x + d, 4)
        receive(dkr.at[there], dc_r.at[d], dc_s.at[d])
        t1[there] = (dkp[k, there].astype(F32) + dkr[there].astype(F32)).astype(BF)
        if d:
            send(t1.at[there], xr.at[d], dx_s.at[d], dx_r.at[d], at_x(d))
    for d in (1, 3, 2):
        receive(xr.at[d], dx_r.at[d], dx_s.at[d])
    t2[...] = (
        t1[x].astype(F32) + xr[1].astype(F32) + xr[2].astype(F32) + xr[3].astype(F32)
    ).astype(BF)
    for e in range(1, 8):
        to = lax.rem(w + e, 8)
        send(
            t2.at[lax.rem(to, 4), lax.div(to, 4)], zr.at[e], dz_s.at[e], dz_r.at[e], at_run(e)
        )

    for d in (1, 3, 2):
        receive(dqg.at[x, lax.rem(zl + 4 - d, 4)], qz_r.at[d], qz_s.at[d])
    for d in (1, 3, 2):
        send(dqg.at[x], dqg.at[x], qx_s.at[d], qx_r.at[d], at_x(d))
    send(dqg.at[x, :, 1 - k], dqp.at[x], qc_s.at[0], qc_r.at[0], mate)

    for d in (1, 3, 2):
        there = lax.rem(y + 4 - d, 4)
        block = xg.at[there, :, k]
        receive(block, xy_r.at[d], xy_s.at[d])
        send(block, block, xc_s.at[d], xc_r.at[d], mate)

    for e in range(1, 8):
        receive(zr.at[e], dz_r.at[e], dz_s.at[e])
    summed = t2[zl, h].astype(F32)
    for e in range(1, 8):
        summed = summed + zr[e].astype(F32)
    here = pl.multiple_of(k * HALF, HALF)
    cosine, sine = cos_ref[pl.ds(here, HALF), :], sin_ref[pl.ds(here, HALF), :]
    first, second = unrotate(summed[:, :64], summed[:, 64:], cosine, sine)
    turned = jnp.concatenate([first, second], axis=1)
    cb[h, k] = jnp.where(h == 0, turned, summed).astype(BF)
    block = cb.at[h, k]
    send(block, block, cx_s.at[0], cx_r.at[0], mate)
    send(block, block, cx_s.at[1], cx_r.at[1], across)
    send(block, block, cx_s.at[2], cx_r.at[2], diagonal)
    receive(cb.at[h, 1 - k], cx_r.at[0], cx_s.at[0])
    receive(cb.at[1 - h, k], cx_r.at[1], cx_s.at[1])
    receive(cb.at[1 - h, 1 - k], cx_r.at[2], cx_s.at[2])
    source = lax.broadcasted_iota(jnp.int32, (128, 128), 0)
    target = lax.broadcasted_iota(jnp.int32, (128, 128), 1)
    wanted = (h * 2 + k) * 32 + lax.rem(target, 32)
    packed = jnp.zeros((HALF, 128), F32)
    for half in range(2):
        for which in range(2):
            group = half * 2 + which
            pick = jnp.where((source == wanted) & (lax.div(target, 32) == group), 1.0, 0.0).astype(BF)
            packed = packed + dot(cb[which, half], pick)
    pg[x, zl] = packed.astype(BF)
    for d in (1, 3, 2):
        block = pg.at[x, zl]
        send(block, block, pz_s.at[d], pz_r.at[d], at_zl(d))
    for d in (1, 3, 2):
        receive(pg.at[x, lax.rem(zl + 4 - d, 4)], pz_r.at[d], pz_s.at[d])
    for d in (1, 3, 2):
        send(pg.at[x], pg.at[x], px_s.at[d], px_r.at[d], at_x(d))
    send(pg.at[x], pgp.at[x], pc_s.at[0], pc_r.at[0], mate)

    for d in (1, 3, 2):
        there = lax.rem(x + 4 - d, 4)
        receive(dqg.at[there], qx_r.at[d], qx_s.at[d])
        send(dqg.at[there, :, 1 - k], dqp.at[there], qc_s.at[d], qc_r.at[d], mate)
    for d in (1, 3, 2):
        there = lax.rem(x + 4 - d, 4)
        receive(pg.at[there], px_r.at[d], px_s.at[d])
        send(pg.at[there], pgp.at[there], pc_s.at[d], pc_r.at[d], mate)
    receive(wqtp, w_r.at[0], w_s.at[0])
    receive(wkvp, w_r.at[1], w_s.at[1])
    for d in (0, 1, 3, 2):
        there = lax.rem(x + 4 - d, 4)
        receive(dqp.at[there], qc_r.at[d], qc_s.at[d])
        receive(pgp.at[there], pc_r.at[d], pc_s.at[d])

    mine = lax.div(lax.broadcasted_iota(jnp.int32, (128, 512), 0), 64) == k
    own_kv = jnp.where(mine, wkv[...].astype(F32), 0.0).astype(BF)
    mate_kv = jnp.where(mine, wkvp[...].astype(F32), 0.0).astype(BF)
    wka[...] = own_kv
    wkb[...] = mate_kv
    for d in (1, 3, 2, 0):
        there = lax.rem(y + d, 4)

        def input_step(i, _):
            part = (
                dot(dqg[there, i, k], wqt[...])
                + dot(dqp[there, i], wqtp[...])
                + dot(pg[there, i], wka[...])
                + dot(pgp[there, i], wkb[...])
            )
            gi[there, i] = part.astype(BF)
            return 0

        lax.fori_loop(0, 4, input_step, 0)
        if d:
            send(gi.at[there], gyr.at[d], gy_s.at[d], gy_r.at[d], at_y(d))

    for d in (0, 1, 3, 2):
        there = lax.rem(y + 4 - d, 4)
        receive(xg.at[there, :, 1 - k], xc_r.at[d], xc_s.at[d])
    accq[...] = jnp.zeros_like(accq)
    acck[...] = jnp.zeros_like(acck)

    def weight_step(i, _):
        b0, b1 = lax.div(i, 4), lax.rem(i, 4)
        accq[...] += dot_first(
            xg[b0, b1].reshape(TOK, 512), dqg[b0, b1].reshape(TOK, 256)
        )
        for half in range(2):
            acck[half] += dot_first(xg[b0, b1, half], pg[b0, b1])
        return 0

    def weight_part(first, last):
        lax.fori_loop(first, last, weight_step, 0)

    weight_part(0, 8)
    for d in (1, 3, 2):
        receive(gyr.at[d], gy_r.at[d], gy_s.at[d])

    def y_sum(i, _):
        gys[i] = (
            gi[y, i].astype(F32)
            + gyr[1, i].astype(F32)
            + gyr[2, i].astype(F32)
            + gyr[3, i].astype(F32)
        ).astype(BF)
        return 0

    lax.fori_loop(0, 4, y_sum, 0)
    for d in (1, 3, 2):
        send(gys.at[lax.rem(zh + d, 4)], gzr.at[d], gz_s.at[d], gz_r.at[d], at_zh(d))
    weight_part(8, 16)
    gwq_ref[...] = accq[...]
    gwk_ref[...] = acck[0][:, 0:32] + acck[1][:, 64:96]
    gwv_ref[...] = acck[0][:, 32:64] + acck[1][:, 96:128]
    for d in (1, 3, 2):
        receive(gzr.at[d], gz_r.at[d], gz_s.at[d])
    gi_ref[...] = (
        gys[zh].astype(F32) + gzr[1].astype(F32) + gzr[2].astype(F32) + gzr[3].astype(F32)
    ).astype(BF)
    for copy in pending:
        copy.wait_send()


def shards(
    layer_input, w_query, w_key, w_value, query, key, value, context_gradient, positions, segments
):
    half_width = HEAD // 2
    freq = jnp.exp(
        -(2.0 * jnp.arange(half_width, dtype=F32) / HEAD) * math.log(ROPE_BASE)
    )
    angle = positions.astype(F32)[:, None] * freq[None, :]
    vmem = pl.BlockSpec(memory_space=pltpu.VMEM)
    b = lambda *shape: pltpu.VMEM(shape, BF)
    f = lambda *shape: pltpu.VMEM(shape, F32)
    scratch = [
        b(2, 4, 8, 96, 128), b(16, TOK, 128), b(16, TOK, 128),
        f(16, TOK, LANES), f(16, TOK, LANES),
        b(128, LANES), b(128, LANES), b(LANES, 128), b(LANES, 128),
        b(256, 512), b(256, 512), b(128, 512), b(128, 512), b(128, 512), b(128, 512), f(128, LANES),
        b(2, 4, 4, 2, HALF, 128), b(4, 4, 2, HALF, 128), b(4, 4, 2, HALF, 128),
        b(4, 4, 2, HALF, 128), b(4, 2, HALF, 128), b(8, HALF, 128), b(2, 2, HALF, 128),
        b(4, 4, HALF, 128), b(4, 4, HALF, 128),
        b(4, 4, 2, HALF, 256), b(4, 4, HALF, 256), b(4, 4, 2, HALF, 512),
        b(4, 4, HALF, 512), b(4, 4, HALF, 512), b(4, HALF, 512), b(4, HALF, 512),
        f(512, 256), f(2, 512, 128),
    ]
    sizes = [8, 4, 4, 2, 4, 4, 4, 4, 4, 8, 3, 4, 4, 4, 4, 4, 4, 4, 4]
    for size in sizes:
        scratch += [pltpu.SemaphoreType.DMA((size,)), pltpu.SemaphoreType.DMA((size,))]
    return pl.pallas_call(
        kernel,
        out_shape=(
            jax.ShapeDtypeStruct((HALF, 512), BF),
            jax.ShapeDtypeStruct((512, 256), F32),
            jax.ShapeDtypeStruct((512, 32), F32),
            jax.ShapeDtypeStruct((512, 32), F32),
        ),
        in_specs=[vmem] * 11,
        out_specs=(vmem,) * 4,
        scratch_shapes=scratch,
        compiler_params=pltpu.CompilerParams(
            collective_id=0, has_side_effects=True, vmem_limit_bytes=48 * 2**20
        ),
        name="attention_backward",
    )(
        layer_input, w_query, w_key, w_value, query, key, value, context_gradient,
        segments.reshape(1, TOK), jnp.cos(angle), jnp.sin(angle),
    )


def solution(mesh):
    return jax.shard_map(
        shards,
        mesh=mesh,
        in_specs=(P("col", "row"),) + (P("row", "col"),) * 7 + (P("row"),) * 2,
        out_specs=(P("col", "row"), P("row", "col"), P("row", "col"), P("row", "col")),
        check_vma=False,
    )
```

```python
import math

import jax
import jax.numpy as jnp
from jax import lax
from jax.experimental import pallas as pl
from jax.experimental.pallas import tpu as pltpu
from jax.sharding import PartitionSpec as P

MESH = pl.DeviceIdType.MESH
BF = jnp.bfloat16
F32 = jnp.float32
HEAD = 128
TOK = 160
HALF = 80
LANES = 384
ROPE_BASE = 500000.0
SCALE = HEAD ** (-0.5)
RUN = (4, 5, 3, 6, 2, 7, 1)


def dot(a, b):
    return lax.dot_general(a, b, (((1,), (0,)), ((), ())), preferred_element_type=F32)


def dot_first(a, b):
    return lax.dot_general(a, b, (((0,), (0,)), ((), ())), preferred_element_type=F32)


def unrotate(first, second, cosine, sine):
    return first * cosine + second * sine, second * cosine - first * sine


def kernel(
    x_ref, wq_ref, wk_ref, wv_ref, q_ref, k_ref, v_ref, o_ref, pos_ref, seg_ref,
    gi_ref, gwq_ref, gwk_ref, gwv_ref,
    kv, meta, cosine, sine, perm, kf, vf, sc, dw, ds, qt, ot, qr, orow, wqt, wqtp, wkv, wkvp, wka, wkb, dqacc,
    dkp, dkr, t1, xr, t2, zr, cb, pg, pgp, dqg, dqp, xg, gi, gyr, gys, gzr, accq, acck,
    mz_s, mz_r, mx_s, mx_r, kz_s, kz_r, kx_s, kx_r, kc_s, kc_r, w_s, w_r,
    xz_s, xz_r, xy_s, xy_r, xc_s, xc_r,
    dc_s, dc_r, dx_s, dx_r, dz_s, dz_r, cx_s, cx_r, pz_s, pz_r, px_s, px_r, pc_s, pc_r,
    qz_s, qz_r, qx_s, qx_r, qc_s, qc_r, gy_s, gy_r, gz_s, gz_r,
):
    row, col = lax.axis_index("row"), lax.axis_index("col")
    x, zl = lax.div(row, 4), lax.rem(row, 4)
    y, zh, k = lax.div(col, 8), lax.rem(lax.div(col, 2), 4), lax.rem(col, 2)
    pair, h = lax.div(zh, 2), lax.rem(zh, 2)
    w = h * 4 + zl

    def device(x_=x, zl_=zl, y_=y, zh_=zh, k_=k):
        return (x_ * 4 + zl_, y_ * 8 + zh_ * 2 + k_)

    def at_x(d):
        return device(x_=lax.rem(x + d, 4))

    def at_y(d):
        return device(y_=lax.rem(y + d, 4))

    def at_zh(d):
        return device(zh_=lax.rem(zh + d, 4))

    def at_zl(d):
        return device(zl_=lax.rem(zl + d, 4))

    def at_run(e):
        there = lax.rem(w + e, 8)
        return device(zl_=lax.rem(there, 4), zh_=pair * 2 + lax.div(there, 4))

    mate = device(k_=1 - k)
    across = device(zh_=pair * 2 + 1 - h)
    far = [device(zh_=(1 - pair) * 2 + i) for i in range(2)]

    pending = []

    def send(src, dst, s_sem, r_sem, to):
        copy = pltpu.make_async_remote_copy(
            src_ref=src, dst_ref=dst, send_sem=s_sem, recv_sem=r_sem,
            device_id=to, device_id_type=MESH,
        )
        copy.start()
        pending.append(copy)

    def receive(dst, r_sem, s_sem):
        pltpu.make_async_remote_copy(
            src_ref=dst, dst_ref=dst, send_sem=s_sem, recv_sem=r_sem,
            device_id=mate, device_id_type=MESH,
        ).wait_recv()

    barrier = pltpu.get_barrier_semaphore()
    peers = [mate] + far
    peers += [at_x(d) for d in (1, 2, 3)] + [at_y(d) for d in (1, 2, 3)]
    peers += [at_run(e) for e in range(1, 8)]
    for peer in peers:
        pl.semaphore_signal(barrier, inc=1, device_id=peer, device_id_type=MESH)

    both = jnp.concatenate([k_ref[...], v_ref[...]], axis=0).astype(F32).T
    kv[k, x, w] = jnp.concatenate([both[:HALF], both[HALF:]], axis=1).astype(BF)
    first_count = jnp.sum(jnp.where(seg_ref[...] == 0, 1.0, 0.0), axis=1, keepdims=True)
    high = lax.div(pos_ref[...], 64)
    low = pos_ref[...] - high * 64
    line = lax.broadcasted_iota(jnp.int32, (16, TOK), 0)
    facts = jnp.where(line == 0, first_count, jnp.where(line == 1, high.astype(F32), low.astype(F32)))
    meta[x, zl, :, 0:TOK] = facts.astype(BF)
    meta[x, zl, :, TOK:256] = jnp.zeros((16, 256 - TOK), BF)
    xg[y, zh, k] = x_ref[...]

    pl.semaphore_wait(barrier, len(peers))

    block = kv.at[k, x, w]
    for d in (2, 1, 3):
        send(block, block, kz_s.at[d], kz_r.at[d], at_zl(d))
    send(block, block, kz_s.at[4], kz_r.at[4], across)
    block = meta.at[x, zl]
    for d in (2, 1, 3):
        send(block, block, mz_s.at[d], mz_r.at[d], at_zl(d))
    block = kv.at[k, x, w]
    for d in (2, 1, 3):
        send(block, block, kx_s.at[d * 8], kx_r.at[d * 8], at_x(d))

    kv_weights = jnp.concatenate([wk_ref[...], wv_ref[...]], axis=0)
    wkv[...] = jnp.concatenate([kv_weights, kv_weights], axis=0)
    wqt[...] = wq_ref[...].astype(F32).T.astype(BF)
    send(wqt, wqtp, w_s.at[0], w_r.at[0], mate)
    send(wkv, wkvp, w_s.at[1], w_r.at[1], mate)
    for i in range(2):
        qr[i * TOK : (i + 1) * TOK] = q_ref[:, i * 128 : (i + 1) * 128]
        orow[i * TOK : (i + 1) * TOK] = o_ref[:, i * 128 : (i + 1) * 128]
    qr[2 * TOK : LANES] = jnp.zeros((LANES - 2 * TOK, 128), BF)
    orow[2 * TOK : LANES] = jnp.zeros((LANES - 2 * TOK, 128), BF)
    qt[...] = qr[...].astype(F32).T.astype(BF)
    ot[...] = orow[...].astype(F32).T.astype(BF)
    source = lax.broadcasted_iota(jnp.int32, (256, 256), 0)
    target = lax.broadcasted_iota(jnp.int32, (256, 256), 1)
    wanted = lax.rem(lax.div(target, 32), 2) * 128 + lax.div(target, 64) * 32 + lax.rem(target, 32)
    perm[...] = jnp.where(source == wanted, 1.0, 0.0).astype(BF)

    def run_block(e):
        if e < 4:
            return kv.at[k, x, h * 4 + lax.rem(zl + 4 - e, 4)]
        return kv.at[k, x, (1 - h) * 4 + lax.rem(zl + 8 - e, 4)]

    for e in (1, 3, 2, 4):
        block = run_block(e)
        receive(block, kz_r.at[e], kz_s.at[e])
        if e == 4:
            for d in (2, 1, 3):
                send(block, block, kz_s.at[4 + d], kz_r.at[4 + d], at_zl(d))
        for d in (2, 1, 3):
            send(block, block, kx_s.at[d * 8 + e], kx_r.at[d * 8 + e], at_x(d))
    for d in (1, 3, 2):
        receive(meta.at[x, lax.rem(zl + 4 - d, 4)], mz_r.at[d], mz_s.at[d])
    for d in (1, 3, 2):
        send(meta.at[x], meta.at[x], mx_s.at[d], mx_r.at[d], at_x(d))
    place = lax.broadcasted_iota(jnp.int32, (64, TOK), 0).astype(F32)
    freq = jnp.exp(-(2.0 * place / HEAD) * math.log(ROPE_BASE))

    def tables(i, _):
        facts = meta[x, i].astype(F32)
        angle = (facts[1:2, 0:TOK] * 64.0 + facts[2:3, 0:TOK]) * freq
        cosine[i] = jnp.cos(angle).T
        sine[i] = jnp.sin(angle).T
        return 0

    lax.fori_loop(0, 4, tables, 0)
    for e in (5, 7, 6):
        block = run_block(e)
        receive(block, kz_r.at[e], kz_s.at[e])
        for d in (2, 1, 3):
            send(block, block, kx_s.at[d * 8 + e], kx_r.at[d * 8 + e], at_x(d))
    send(kv.at[k, x], kv.at[k, x], kc_s.at[0], kc_r.at[0], mate)
    block = xg.at[y, zh, k]
    for d in (2, 1, 3):
        send(block, block, xz_s.at[d], xz_r.at[d], at_zh(d))

    for d in (1, 3, 2):
        receive(meta.at[lax.rem(x + 4 - d, 4)], mx_r.at[d], mx_s.at[d])
    cut = jnp.zeros((1, 1), F32)
    for xx in range(4):
        for zz in range(4):
            cut = cut + meta[xx, zz].astype(F32)[0:1, 0:1]
    lane = lax.broadcasted_iota(jnp.int32, (1, LANES), 1)
    query = lane - TOK * (lane >= TOK).astype(jnp.int32) - TOK * (lane >= 2 * TOK).astype(jnp.int32)
    query = query + row * TOK
    cut = jnp.broadcast_to(cut, (1, LANES)).astype(jnp.int32)
    begin = jnp.where(query < cut, 0, cut)

    def products(there, peak):
        def step(i, peak):
            at = there * 4 + i
            for half in range(2):
                parts = [kv[kk, there, hh * 4 + i] for hh in range(2) for kk in range(2)]
                lo = 64 * half
                kf[at, half * HALF : (half + 1) * HALF, :] = jnp.concatenate(
                    [p[:, lo : lo + 32] for p in parts], axis=1
                )
                vf[at, half * HALF : (half + 1) * HALF, :] = jnp.concatenate(
                    [p[:, lo + 32 : lo + 64] for p in parts], axis=1
                )
            dw[at] = dot(vf[at], ot[...])
            key = at * TOK + lax.broadcasted_iota(jnp.int32, (TOK, LANES), 0)
            seen = (key >= begin) & (key <= query)
            seen = jnp.where(seen, dot(kf[at], qt[...]) * SCALE, -1e30)
            sc[at] = seen
            return jnp.maximum(peak, jnp.max(seen, axis=0, keepdims=True))

        return lax.fori_loop(0, 4, step, peak)

    receive(kv.at[1 - k, x], kc_r.at[0], kc_s.at[0])
    peak = products(x, jnp.full((1, LANES), -1e30, F32))
    for d in (1, 3, 2):
        there = lax.rem(x + 4 - d, 4)
        for e in range(8):
            at = h * 4 + lax.rem(zl + 4 - e, 4) if e < 4 else (1 - h) * 4 + lax.rem(zl + 8 - e, 4)
            block = kv.at[k, there, at]
            receive(block, kx_r.at[d * 8 + e], kx_s.at[d * 8 + e])
        send(kv.at[k, there], kv.at[k, there], kc_s.at[d], kc_r.at[d], mate)
    for d in (1, 3, 2):
        there = lax.rem(x + 4 - d, 4)
        receive(kv.at[1 - k, there], kc_r.at[d], kc_s.at[d])
        peak = products(there, peak)


    def sum_step(b, sums):
        total, delta = sums
        term = jnp.exp(sc[b] - peak)
        sc[b] = term
        return (
            total + jnp.sum(term, axis=0, keepdims=True),
            delta + jnp.sum(term * dw[b], axis=0, keepdims=True),
        )

    zero = jnp.zeros((1, LANES), F32)
    total, delta = lax.fori_loop(0, 16, sum_step, (zero, zero))
    inverse = 1.0 / total
    delta = delta * inverse

    dqacc[...] = jnp.zeros_like(dqacc)
    cosines, sines = cosine[zl], sine[zl]

    def key_sum(d):
        there = lax.rem(x + d, 4)
        receive(dkr.at[there], dc_r.at[d], dc_s.at[d])
        t1[there] = (dkp[k, there].astype(F32) + dkr[there].astype(F32)).astype(BF)
        if d:
            send(t1.at[there], xr.at[d], dx_s.at[d], dx_r.at[d], at_x(d))

    before = None
    for d in (2, 1, 3, 0):
        there = lax.rem(x + d, 4)

        def grad_step(i, _):
            b = there * 4 + i
            weights = sc[b] * inverse
            dscores = (weights * (dw[b] - delta) * SCALE).astype(BF)
            ds[i] = dscores
            dkey = dot(dscores, qr[...]).astype(BF)
            dvalue = dot(weights.astype(BF), orow[...]).astype(BF)
            for half in range(2):
                dkp[half, there, i, 0] = dkey[half * HALF : (half + 1) * HALF]
                dkp[half, there, i, 1] = dvalue[half * HALF : (half + 1) * HALF]
            return 0

        lax.fori_loop(0, 4, grad_step, 0)
        send(dkp.at[1 - k, there], dkr.at[there], dc_s.at[d], dc_r.at[d], mate)
        dqacc[...] += dot_first(
            kf[pl.ds(there * 4, 4)].reshape(4 * TOK, HEAD), ds[...].reshape(4 * TOK, LANES)
        )
        if before is not None:
            key_sum(before)
        before = d

    dquery = dqacc[...].T
    for head in range(2):
        part = dquery[head * TOK : (head + 1) * TOK]
        first, second = unrotate(part[:, :64], part[:, 64:], cosines, sines)
        both = jnp.concatenate([first, second], axis=1).astype(BF)
        for half in range(2):
            dqg[x, zl, half, :, head * 128 : (head + 1) * 128] = both[half * HALF : (half + 1) * HALF]
    block = dqg.at[x, zl]
    for d in (1, 3, 2):
        send(block, block, qz_s.at[d], qz_r.at[d], at_zl(d))
    key_sum(0)
    for d in (1, 3, 2):
        receive(xg.at[y, lax.rem(zh + 4 - d, 4), k], xz_r.at[d], xz_s.at[d])
    block = xg.at[y, :, k]
    for d in (2, 1, 3):
        send(block, block, xy_s.at[d], xy_r.at[d], at_y(d))
    send(block, block, xc_s.at[0], xc_r.at[0], mate)
    for d in (1, 3, 2):
        receive(xr.at[d], dx_r.at[d], dx_s.at[d])
    here = pl.multiple_of(k * HALF, HALF)

    def x_sum(i, _):
        total = t1[x, i].astype(F32)
        for d in range(1, 4):
            total = total + xr[d, i].astype(F32)
        first, second = unrotate(
            total[0, :, :64], total[0, :, 64:],
            cosine[i, pl.ds(here, HALF), :], sine[i, pl.ds(here, HALF), :],
        )
        wide = jnp.concatenate([first, second, total[1]], axis=1).astype(BF)
        wide = dot(wide, perm[...]).astype(BF)
        t2[i, 0] = wide[:, :128]
        t2[i, 1] = wide[:, 128:]
        return 0

    lax.fori_loop(0, 4, x_sum, 0)
    for e in RUN:
        to = lax.rem(w + e, 8)
        send(
            t2.at[lax.rem(to, 4), lax.div(to, 4)], zr.at[e], dz_s.at[e], dz_r.at[e], at_run(e)
        )

    for d in (1, 3, 2):
        receive(dqg.at[x, lax.rem(zl + 4 - d, 4)], qz_r.at[d], qz_s.at[d])
    for d in (2, 1, 3):
        send(dqg.at[x], dqg.at[x], qx_s.at[d], qx_r.at[d], at_x(d))
    send(dqg.at[x, :, 1 - k], dqp.at[x], qc_s.at[0], qc_r.at[0], mate)

    for d in (1, 3, 2):
        there = lax.rem(y + 4 - d, 4)
        block = xg.at[there, :, k]
        receive(block, xy_r.at[d], xy_s.at[d])
        send(block, block, xc_s.at[d], xc_r.at[d], mate)

    for e in range(1, 8):
        receive(zr.at[e], dz_r.at[e], dz_s.at[e])
    summed = t2[zl, h].astype(F32)
    for e in range(1, 8):
        summed = summed + zr[e].astype(F32)
    cb[k] = summed.astype(BF)
    send(cb.at[k], cb.at[k], cx_s.at[0], cx_r.at[0], mate)
    receive(cb.at[1 - k], cx_r.at[0], cx_s.at[0])
    halves = [
        jnp.concatenate([cb[0][:, lo : lo + 64], cb[1][:, lo : lo + 64]], axis=1) for lo in (0, 64)
    ]
    pg[x, zl] = jnp.where(k == 0, halves[0].astype(F32), halves[1].astype(F32)).astype(BF)
    for d in (1, 3, 2):
        block = pg.at[x, zl]
        send(block, block, pz_s.at[d], pz_r.at[d], at_zl(d))
    for d in (1, 3, 2):
        receive(pg.at[x, lax.rem(zl + 4 - d, 4)], pz_r.at[d], pz_s.at[d])
    for d in (1, 3, 2):
        send(pg.at[x], pg.at[x], px_s.at[d], px_r.at[d], at_x(d))
    send(pg.at[x], pgp.at[x], pc_s.at[0], pc_r.at[0], mate)

    for d in (1, 3, 2):
        there = lax.rem(x + 4 - d, 4)
        receive(dqg.at[there], qx_r.at[d], qx_s.at[d])
        send(dqg.at[there, :, 1 - k], dqp.at[there], qc_s.at[d], qc_r.at[d], mate)
    for d in (1, 3, 2):
        there = lax.rem(x + 4 - d, 4)
        receive(pg.at[there], px_r.at[d], px_s.at[d])
        send(pg.at[there], pgp.at[there], pc_s.at[d], pc_r.at[d], mate)
    receive(wqtp, w_r.at[0], w_s.at[0])
    receive(wkvp, w_r.at[1], w_s.at[1])
    for d in (0, 1, 3, 2):
        there = lax.rem(x + 4 - d, 4)
        receive(dqp.at[there], qc_r.at[d], qc_s.at[d])
        receive(pgp.at[there], pc_r.at[d], pc_s.at[d])

    mine = lax.div(lax.broadcasted_iota(jnp.int32, (128, 512), 0), 64) == k
    own_kv = jnp.where(mine, wkv[...].astype(F32), 0.0).astype(BF)
    mate_kv = jnp.where(mine, wkvp[...].astype(F32), 0.0).astype(BF)
    wka[...] = own_kv
    wkb[...] = mate_kv
    def input_part(c):
        part = slice(c * 128, (c + 1) * 128)

        def input_step(there, _):
            gi[c, there] = (
                (
                    dot(dqg[there, :, k].reshape(4 * HALF, 256), wqt[:, part])
                    + dot(dqp[there].reshape(4 * HALF, 256), wqtp[:, part])
                    + dot(pg[there].reshape(4 * HALF, 128), wka[:, part])
                    + dot(pgp[there].reshape(4 * HALF, 128), wkb[:, part])
                )
                .astype(BF)
                .reshape(4, HALF, 128)
            )
            return 0

        lax.fori_loop(0, 4, input_step, 0)

    def input_send(c):
        for d in (2, 1, 3):
            send(
                gi.at[c, lax.rem(y + d, 4)], gyr.at[c, d],
                gy_s.at[c * 4 + d], gy_r.at[c * 4 + d], at_y(d),
            )

    for c in range(4):
        input_part(c)
        if c < 2:
            input_send(c)

    for d in (0, 1, 3, 2):
        there = lax.rem(y + 4 - d, 4)
        receive(xg.at[there, :, 1 - k], xc_r.at[d], xc_s.at[d])
    accq[...] = jnp.zeros_like(accq)
    acck[...] = jnp.zeros_like(acck)

    def weight_step(i, _):
        b0, b1 = lax.div(i, 4), lax.rem(i, 4)
        accq[...] += dot_first(xg[b0, b1].reshape(TOK, 512), dqg[b0, b1].reshape(TOK, 256))
        for half in range(2):
            acck[half] += dot_first(pg[b0, b1], xg[b0, b1, half])
        return 0

    def weight_part(first, last):
        lax.fori_loop(first, last, weight_step, 0)

    weight_part(0, 4)
    for c in range(4):
        for d in (1, 3, 2):
            receive(gyr.at[c, d], gy_r.at[c * 4 + d], gy_s.at[c * 4 + d])
        if c < 2:
            input_send(c + 2)
        gys[c] = (
            gi[c, y].astype(F32)
            + gyr[c, 1].astype(F32)
            + gyr[c, 2].astype(F32)
            + gyr[c, 3].astype(F32)
        ).astype(BF)
        for d in (2, 1, 3):
            send(
                gys.at[c, lax.rem(zh + d, 4)], gzr.at[c, d],
                gz_s.at[c * 4 + d], gz_r.at[c * 4 + d], at_zh(d),
            )
        if c < 3:
            weight_part(4 + c * 3, 7 + c * 3)
    weight_part(13, 16)
    gwq_ref[...] = accq[...]
    gwk_ref[...] = acck[0, 0:32] + acck[1, 64:96]
    gwv_ref[...] = acck[0, 32:64] + acck[1, 96:128]
    for c in range(4):
        for d in (1, 3, 2):
            receive(gzr.at[c, d], gz_r.at[c * 4 + d], gz_s.at[c * 4 + d])
        gi_ref[:, c * 128 : (c + 1) * 128] = (
            gys[c, zh].astype(F32)
            + gzr[c, 1].astype(F32)
            + gzr[c, 2].astype(F32)
            + gzr[c, 3].astype(F32)
        ).astype(BF)
    for copy in pending:
        copy.wait_send()


def shards(
    layer_input, w_query, w_key, w_value, query, key, value, context_gradient, positions, segments
):
    vmem = pl.BlockSpec(memory_space=pltpu.VMEM)
    b = lambda *shape: pltpu.VMEM(shape, BF)
    f = lambda *shape: pltpu.VMEM(shape, F32)
    scratch = [
        b(2, 4, 8, HALF, 128), b(4, 4, 16, 256), f(4, TOK, 64), f(4, TOK, 64), b(256, 256),
        b(16, TOK, 128), b(16, TOK, 128), f(16, TOK, LANES), f(16, TOK, LANES), b(4, TOK, LANES),
        b(128, LANES), b(128, LANES), b(LANES, 128), b(LANES, 128),
        b(256, 512), b(256, 512), b(128, 512), b(128, 512), b(128, 512), b(128, 512), f(128, LANES),
        b(2, 4, 4, 2, HALF, 128), b(4, 4, 2, HALF, 128), b(4, 4, 2, HALF, 128),
        b(4, 4, 2, HALF, 128), b(4, 2, HALF, 128), b(8, HALF, 128), b(2, HALF, 128),
        b(4, 4, HALF, 128), b(4, 4, HALF, 128),
        b(4, 4, 2, HALF, 256), b(4, 4, HALF, 256), b(4, 4, 2, HALF, 512),
        b(4, 4, 4, HALF, 128), b(4, 4, 4, HALF, 128), b(4, 4, HALF, 128), b(4, 4, HALF, 128),
        f(512, 256), f(2, 128, 512),
    ]
    sizes = [4, 4, 8, 32, 4, 2, 4, 4, 4, 4, 4, 8, 1, 4, 4, 4, 4, 4, 4, 16, 16]
    for size in sizes:
        scratch += [pltpu.SemaphoreType.DMA((size,)), pltpu.SemaphoreType.DMA((size,))]
    gi, gwq, gwk, gwv = pl.pallas_call(
        kernel,
        out_shape=(
            jax.ShapeDtypeStruct((HALF, 512), BF),
            jax.ShapeDtypeStruct((512, 256), F32),
            jax.ShapeDtypeStruct((32, 512), F32),
            jax.ShapeDtypeStruct((32, 512), F32),
        ),
        in_specs=[vmem] * 10,
        out_specs=(vmem,) * 4,
        scratch_shapes=scratch,
        compiler_params=pltpu.CompilerParams(
            collective_id=0, has_side_effects=True, vmem_limit_bytes=48 * 2**20
        ),
        name="attention_backward",
    )(
        layer_input, w_query, w_key.T, w_value.T, query, key.T, value.T, context_gradient,
        positions.reshape(1, TOK), segments.reshape(1, TOK),
    )
    return gi, gwq, gwk.T, gwv.T


def solution(mesh):
    return jax.shard_map(
        shards,
        mesh=mesh,
        in_specs=(P("col", "row"),) + (P("row", "col"),) * 7 + (P("row"),) * 2,
        out_specs=(P("col", "row"), P("row", "col"), P("row", "col"), P("row", "col")),
        check_vma=False,
    )
```

```python
import math

import jax
import jax.numpy as jnp
from jax import lax
from jax.experimental import pallas as pl
from jax.experimental.pallas import tpu as pltpu
from jax.sharding import PartitionSpec as P

MESH = pl.DeviceIdType.MESH
BF = jnp.bfloat16
F32 = jnp.float32
HEAD = 128
TOK = 160
HALF = 80
LANES = 384
ROPE_BASE = 500000.0
VMEM_BYTES = 127 * 2**19
SCALE = HEAD ** (-0.5)
RUN = (4, 5, 3, 6, 2, 7, 1)
ROWS = (pl.ds(0, 48), pl.ds(48, 32))


def dot(a, b):
    return lax.dot_general(a, b, (((1,), (0,)), ((), ())), preferred_element_type=F32)


def dot_first(a, b):
    return lax.dot_general(a, b, (((0,), (0,)), ((), ())), preferred_element_type=F32)


def unrotate(first, second, cosine, sine):
    return first * cosine + second * sine, second * cosine - first * sine


def kernel(
    x_hbm, wq_hbm, wk_hbm, wv_hbm, q_hbm, k_hbm, v_hbm, o_hbm, pos_hbm, seg_hbm,
    gi_ref, gwq_ref, gwk_ref, gwv_ref,
    wq_ref, wk_ref, wv_ref, q_ref, k_ref, v_ref, o_ref, pos_ref, seg_ref,
    kv, meta, cosine, sine, perm, kf, vf, sc, dw, ds, qt, ot, qr, orow, wqt, wkv, dqacc,
    dkp, dkr, t1, xr, t2, zr, gk, gkm, dqo, dqg, dqm, xg, gi, gyr, gys, gzr, accq, acck,
    load, mz_s, mz_r, mx_s, mx_r, kz_s, kz_r, kx_s, kx_r, kc_s, kc_r, w_s, w_r,
    xz_s, xz_r, xy_s, xy_r, xc_s, xc_r,
    dc_s, dc_r, dx_s, dx_r, dz_s, dz_r, pz_s, pz_r, px_s, px_r, pc_s, pc_r,
    qm_s, qm_r, qz_s, qz_r, qx_s, qx_r, qc_s, qc_r, gy_s, gy_r, gz_s, gz_r,
):
    row, col = lax.axis_index("row"), lax.axis_index("col")
    x, zl = lax.div(row, 4), lax.rem(row, 4)
    y, zh, k = lax.div(col, 8), lax.rem(lax.div(col, 2), 4), lax.rem(col, 2)
    pair, h = lax.div(zh, 2), lax.rem(zh, 2)
    w = h * 4 + zl

    def device(x_=x, zl_=zl, y_=y, zh_=zh, k_=k):
        return (x_ * 4 + zl_, y_ * 8 + zh_ * 2 + k_)

    def at_x(d):
        return device(x_=lax.rem(x + d, 4))

    def at_y(d):
        return device(y_=lax.rem(y + d, 4))

    def at_zh(d):
        return device(zh_=lax.rem(zh + d, 4))

    def at_zl(d):
        return device(zl_=lax.rem(zl + d, 4))

    def at_run(e):
        there = lax.rem(w + e, 8)
        return device(zl_=lax.rem(there, 4), zh_=pair * 2 + lax.div(there, 4))

    mate = device(k_=1 - k)
    across = device(zh_=pair * 2 + 1 - h)
    far = [device(zh_=(1 - pair) * 2 + i) for i in range(2)]

    pending = []

    def send(src, dst, s_sem, r_sem, to):
        copy = pltpu.make_async_remote_copy(
            src_ref=src, dst_ref=dst, send_sem=s_sem, recv_sem=r_sem,
            device_id=to, device_id_type=MESH,
        )
        copy.start()
        pending.append(copy)

    def receive(dst, r_sem, s_sem):
        pltpu.make_async_remote_copy(
            src_ref=dst, dst_ref=dst, send_sem=s_sem, recv_sem=r_sem,
            device_id=mate, device_id_type=MESH,
        ).wait_recv()

    barrier = pltpu.get_barrier_semaphore()
    peers = [mate] + far
    peers += [at_x(d) for d in (1, 2, 3)] + [at_y(d) for d in (1, 2, 3)]
    peers += [at_run(e) for e in range(1, 8)]
    for peer in peers:
        pl.semaphore_signal(barrier, inc=1, device_id=peer, device_id_type=MESH)

    loads = [
        pltpu.make_async_copy(src, dst, load.at[i])
        for i, (src, dst) in enumerate([
            (k_hbm, k_ref), (v_hbm, v_ref), (pos_hbm, pos_ref), (seg_hbm, seg_ref),
            (x_hbm, xg.at[y, zh, k]), (wk_hbm, wk_ref), (wv_hbm, wv_ref), (wq_hbm, wq_ref),
            (q_hbm, q_ref), (o_hbm, o_ref),
        ])
    ]
    for copy in loads:
        copy.start()
    for copy in loads[:4]:
        copy.wait()

    both = jnp.concatenate([k_ref[...], v_ref[...]], axis=0).astype(F32).T
    kv[k, x, w] = jnp.concatenate([both[:HALF], both[HALF:]], axis=1).astype(BF)
    first_count = jnp.sum(jnp.where(seg_ref[...] == 0, 1.0, 0.0), axis=1, keepdims=True)
    high = lax.div(pos_ref[...], 64)
    low = pos_ref[...] - high * 64
    line = lax.broadcasted_iota(jnp.int32, (16, TOK), 0)
    facts = jnp.where(line == 0, first_count, jnp.where(line == 1, high.astype(F32), low.astype(F32)))
    meta[x, zl, :, 0:TOK] = facts.astype(BF)
    meta[x, zl, :, TOK:256] = jnp.zeros((16, 256 - TOK), BF)

    pl.semaphore_wait(barrier, len(peers))

    block = kv.at[k, x, w]
    for d in (2, 1, 3):
        send(block, block, kz_s.at[d], kz_r.at[d], at_zl(d))
    send(block, block, kz_s.at[4], kz_r.at[4], across)
    block = meta.at[x, zl]
    for d in (2, 1, 3):
        send(block, block, mz_s.at[d], mz_r.at[d], at_zl(d))
    block = kv.at[k, x, w]
    for d in (2, 1, 3):
        send(block, block, kx_s.at[d * 8], kx_r.at[d * 8], at_x(d))

    for copy in loads[4:]:
        copy.wait()
    rows = pl.ds(pl.multiple_of(k * 64, 64), 64)
    wkv[rows, :] = jnp.concatenate([wk_ref[...], wv_ref[...]], axis=0)
    send(wkv.at[rows], wkv.at[rows], w_s.at[1], w_r.at[1], mate)
    rows = pl.ds(pl.multiple_of(k * 256, 256), 256)
    wqt[rows, :] = wq_ref[...].astype(F32).T.astype(BF)
    send(wqt.at[rows], wqt.at[rows], w_s.at[0], w_r.at[0], mate)
    for i in range(2):
        qr[i * TOK : (i + 1) * TOK] = q_ref[:, i * 128 : (i + 1) * 128]
        orow[i * TOK : (i + 1) * TOK] = o_ref[:, i * 128 : (i + 1) * 128]
    qr[2 * TOK : LANES] = jnp.zeros((LANES - 2 * TOK, 128), BF)
    orow[2 * TOK : LANES] = jnp.zeros((LANES - 2 * TOK, 128), BF)
    qt[...] = qr[...].astype(F32).T.astype(BF)
    ot[...] = orow[...].astype(F32).T.astype(BF)
    source = lax.broadcasted_iota(jnp.int32, (256, 256), 0)
    target = lax.broadcasted_iota(jnp.int32, (256, 256), 1)
    wanted = lax.rem(lax.div(target, 32), 2) * 128 + lax.div(target, 64) * 32 + lax.rem(target, 32)
    perm[...] = jnp.where(source == wanted, 1.0, 0.0).astype(BF)

    def run_block(e):
        if e < 4:
            return kv.at[k, x, h * 4 + lax.rem(zl + 4 - e, 4)]
        return kv.at[k, x, (1 - h) * 4 + lax.rem(zl + 8 - e, 4)]

    for e in (1, 3, 2, 4):
        block = run_block(e)
        receive(block, kz_r.at[e], kz_s.at[e])
        if e == 4:
            for d in (2, 1, 3):
                send(block, block, kz_s.at[4 + d], kz_r.at[4 + d], at_zl(d))
        for d in (2, 1, 3):
            send(block, block, kx_s.at[d * 8 + e], kx_r.at[d * 8 + e], at_x(d))
    for d in (1, 3, 2):
        receive(meta.at[x, lax.rem(zl + 4 - d, 4)], mz_r.at[d], mz_s.at[d])
    for d in (1, 3, 2):
        send(meta.at[x], meta.at[x], mx_s.at[d], mx_r.at[d], at_x(d))
    place = lax.broadcasted_iota(jnp.int32, (64, TOK), 0).astype(F32)
    freq = jnp.exp(-(2.0 * place / HEAD) * math.log(ROPE_BASE))

    def tables(i, _):
        facts = meta[x, i].astype(F32)
        angle = (facts[1:2, 0:TOK] * 64.0 + facts[2:3, 0:TOK]) * freq
        cosine[i] = jnp.cos(angle).T
        sine[i] = jnp.sin(angle).T
        return 0

    lax.fori_loop(0, 4, tables, 0)
    for e in (5, 7, 6):
        block = run_block(e)
        receive(block, kz_r.at[e], kz_s.at[e])
        for d in (2, 1, 3):
            send(block, block, kx_s.at[d * 8 + e], kx_r.at[d * 8 + e], at_x(d))
    send(kv.at[k, x], kv.at[k, x], kc_s.at[0], kc_r.at[0], mate)
    block = xg.at[y, zh, k]
    for d in (2, 1, 3):
        send(block, block, xz_s.at[d], xz_r.at[d], at_zh(d))

    for d in (1, 3, 2):
        receive(meta.at[lax.rem(x + 4 - d, 4)], mx_r.at[d], mx_s.at[d])
    cut = jnp.zeros((1, 1), F32)
    for xx in range(4):
        for zz in range(4):
            cut = cut + meta[xx, zz].astype(F32)[0:1, 0:1]
    lane = lax.broadcasted_iota(jnp.int32, (1, LANES), 1)
    query = lane - TOK * (lane >= TOK).astype(jnp.int32) - TOK * (lane >= 2 * TOK).astype(jnp.int32)
    query = query + row * TOK
    cut = jnp.broadcast_to(cut, (1, LANES)).astype(jnp.int32)
    begin = jnp.where(query < cut, 0, cut)

    def products(there, peak):
        def step(i, peak):
            at = there * 4 + i
            for half in range(2):
                parts = [kv[kk, there, hh * 4 + i] for hh in range(2) for kk in range(2)]
                lo = 64 * half
                kf[at, half * HALF : (half + 1) * HALF, :] = jnp.concatenate(
                    [p[:, lo : lo + 32] for p in parts], axis=1
                )
                vf[at, half * HALF : (half + 1) * HALF, :] = jnp.concatenate(
                    [p[:, lo + 32 : lo + 64] for p in parts], axis=1
                )
            dw[at] = dot(vf[at], ot[...])
            key = at * TOK + lax.broadcasted_iota(jnp.int32, (TOK, LANES), 0)
            seen = (key >= begin) & (key <= query)
            seen = jnp.where(seen, dot(kf[at], qt[...]) * SCALE, -1e30)
            sc[at] = seen
            return jnp.maximum(peak, jnp.max(seen, axis=0, keepdims=True))

        return lax.fori_loop(0, 4, step, peak)

    receive(kv.at[1 - k, x], kc_r.at[0], kc_s.at[0])
    peak = products(x, jnp.full((1, LANES), -1e30, F32))
    for d in (1, 3, 2):
        there = lax.rem(x + 4 - d, 4)
        for e in range(8):
            at = h * 4 + lax.rem(zl + 4 - e, 4) if e < 4 else (1 - h) * 4 + lax.rem(zl + 8 - e, 4)
            block = kv.at[k, there, at]
            receive(block, kx_r.at[d * 8 + e], kx_s.at[d * 8 + e])
        send(kv.at[k, there], kv.at[k, there], kc_s.at[d], kc_r.at[d], mate)
    for d in (1, 3, 2):
        there = lax.rem(x + 4 - d, 4)
        receive(kv.at[1 - k, there], kc_r.at[d], kc_s.at[d])
        peak = products(there, peak)


    def sum_step(b, sums):
        total, delta = sums
        term = jnp.exp(sc[b] - peak)
        sc[b] = term
        return (
            total + jnp.sum(term, axis=0, keepdims=True),
            delta + jnp.sum(term * dw[b], axis=0, keepdims=True),
        )

    zero = jnp.zeros((1, LANES), F32)
    total, delta = lax.fori_loop(0, 16, sum_step, (zero, zero))
    inverse = 1.0 / total
    delta = delta * inverse

    dqacc[...] = jnp.zeros_like(dqacc)
    cosines, sines = cosine[zl], sine[zl]

    def key_send(d, part):
        there, rows = lax.rem(x + d, 4), ROWS[part]
        send(
            t1.at[there, :, :, rows], xr.at[d, :, :, rows],
            dx_s.at[d * 2 + part], dx_r.at[d * 2 + part], at_x(d),
        )

    def key_sum(d):
        there = lax.rem(x + d, 4)
        receive(dkr.at[there], dc_r.at[d], dc_s.at[d])
        t1[there] = (dkp[k, there].astype(F32) + dkr[there].astype(F32)).astype(BF)
        if d:
            key_send(d, 0)

    before = None
    for d in (2, 1, 3, 0):
        there = lax.rem(x + d, 4)

        def grad_step(i, _):
            b = there * 4 + i
            weights = sc[b] * inverse
            dscores = (weights * (dw[b] - delta) * SCALE).astype(BF)
            ds[i] = dscores
            dkey = dot(dscores, qr[...]).astype(BF)
            dvalue = dot(weights.astype(BF), orow[...]).astype(BF)
            for half in range(2):
                dkp[half, there, i, 0] = dkey[half * HALF : (half + 1) * HALF]
                dkp[half, there, i, 1] = dvalue[half * HALF : (half + 1) * HALF]
            return 0

        lax.fori_loop(0, 4, grad_step, 0)
        send(dkp.at[1 - k, there], dkr.at[there], dc_s.at[d], dc_r.at[d], mate)
        dqacc[...] += dot_first(
            kf[pl.ds(there * 4, 4)].reshape(4 * TOK, HEAD), ds[...].reshape(4 * TOK, LANES)
        )
        if before is not None:
            key_sum(before)
        before = d

    dquery = dqacc[...].T
    for head in range(2):
        part = dquery[head * TOK : (head + 1) * TOK]
        first, second = unrotate(part[:, :64], part[:, 64:], cosines, sines)
        both = jnp.concatenate([first, second], axis=1).astype(BF)
        for half in range(2):
            dqo[half, :, head * 128 : (head + 1) * 128] = both[half * HALF : (half + 1) * HALF]
    mine = pl.ds(pl.multiple_of(k * 256, 256), 256)
    other = pl.ds(pl.multiple_of((1 - k) * 256, 256), 256)
    send(dqo.at[1 - k], dqg.at[x, zl, :, mine], qm_s.at[0], qm_r.at[0], mate)
    dqg[x, zl, :, mine] = dqo[k]
    key_sum(0)
    receive(dqg.at[x, zl, :, other], qm_r.at[0], qm_s.at[0])
    block = dqg.at[x, zl]
    for d in (2, 1, 3):
        send(block, block, qz_s.at[d], qz_r.at[d], at_zl(d))
    for d in (2, 1, 3):
        key_send(d, 1)
    for d in (2, 1, 3):
        send(block, block, qx_s.at[d * 4], qx_r.at[d * 4], at_x(d))

    for d in (1, 3, 2):
        receive(xg.at[y, lax.rem(zh + 4 - d, 4), k], xz_r.at[d], xz_s.at[d])
    block = xg.at[y, :, k]
    for d in (2, 1, 3):
        send(block, block, xy_s.at[d], xy_r.at[d], at_y(d))
    send(block, block, xc_s.at[0], xc_r.at[0], mate)

    def x_sum(part):
        lo, size = (0, 48) if part == 0 else (48, 32)
        at = pl.ds(pl.multiple_of(k * HALF + lo, 16), size)

        def step(i, _):
            total = t1[x, i, :, lo : lo + size].astype(F32)
            for d in range(1, 4):
                total = total + xr[d, i, :, lo : lo + size].astype(F32)
            first, second = unrotate(
                total[0, :, :64], total[0, :, 64:], cosine[i, at, :], sine[i, at, :]
            )
            wide = jnp.concatenate([first, second, total[1]], axis=1).astype(BF)
            wide = dot(wide, perm[...]).astype(BF)
            t2[i, 0, lo : lo + size] = wide[:, :128]
            t2[i, 1, lo : lo + size] = wide[:, 128:]
            return 0

        lax.fori_loop(0, 4, step, 0)

    for part in range(2):
        for d in (1, 3, 2):
            rows = ROWS[part]
            receive(xr.at[d, :, :, rows], dx_r.at[d * 2 + part], dx_s.at[d * 2 + part])
        x_sum(part)
        for e in RUN:
            to = lax.rem(w + e, 8)
            send(
                t2.at[lax.rem(to, 4), lax.div(to, 4), rows], zr.at[e, rows],
                dz_s.at[e * 2 + part], dz_r.at[e * 2 + part], at_run(e),
            )

    for e in (1, 3, 2):
        block = dqg.at[x, lax.rem(zl + 4 - e, 4)]
        receive(block, qz_r.at[e], qz_s.at[e])
        for d in (2, 1, 3):
            send(block, block, qx_s.at[d * 4 + e], qx_r.at[d * 4 + e], at_x(d))

    for part in range(2):
        for e in RUN:
            rows = ROWS[part]
            receive(zr.at[e, rows], dz_r.at[e * 2 + part], dz_s.at[e * 2 + part])
    summed = t2[zl, h].astype(F32)
    for e in range(1, 8):
        summed = summed + zr[e].astype(F32)
    gk[x, zl] = summed.astype(BF)
    block = gk.at[x, zl]
    for d in (2, 1, 3):
        send(block, block, pz_s.at[d], pz_r.at[d], at_zl(d))
    for d in (2, 1, 3):
        send(block, block, px_s.at[d * 4], px_r.at[d * 4], at_x(d))
    for e in (1, 3, 2):
        block = gk.at[x, lax.rem(zl + 4 - e, 4)]
        receive(block, pz_r.at[e], pz_s.at[e])
        for d in (2, 1, 3):
            send(block, block, px_s.at[d * 4 + e], px_r.at[d * 4 + e], at_x(d))

    receive(wqt.at[pl.ds(pl.multiple_of((1 - k) * 256, 256), 256)], w_r.at[0], w_s.at[0])
    receive(wkv.at[pl.ds(pl.multiple_of((1 - k) * 64, 64), 64)], w_r.at[1], w_s.at[1])
    for d in (1, 3, 2):
        there = lax.rem(x + 4 - d, 4)
        for e in range(4):
            block = dqg.at[there, lax.rem(zl + 4 - e, 4)]
            receive(block, qx_r.at[d * 4 + e], qx_s.at[d * 4 + e])
    for d in (1, 3, 2):
        there = lax.rem(x + 4 - d, 4)
        for e in range(4):
            block = gk.at[there, lax.rem(zl + 4 - e, 4)]
            receive(block, px_r.at[d * 4 + e], px_s.at[d * 4 + e])

    def input_part(c):
        part = slice(c * 128, (c + 1) * 128)

        def input_step(there, _):
            gi[c, there] = (
                (
                    dot(dqg[there].reshape(4 * HALF, 512), wqt[:, part])
                    + dot(gk[there].reshape(4 * HALF, 128), wkv[:, part])
                )
                .astype(BF)
                .reshape(4, HALF, 128)
            )
            return 0

        lax.fori_loop(0, 4, input_step, 0)

    def input_send(c):
        for d in (2, 1, 3):
            send(
                gi.at[c, lax.rem(y + d, 4)], gyr.at[c, d],
                gy_s.at[c * 4 + d], gy_r.at[c * 4 + d], at_y(d),
            )

    for c in range(4):
        input_part(c)
        if c < 2:
            input_send(c)

    for d in (1, 3, 2):
        there = lax.rem(y + 4 - d, 4)
        block = xg.at[there, :, k]
        receive(block, xy_r.at[d], xy_s.at[d])
        send(block, block, xc_s.at[d], xc_r.at[d], mate)
    for there in range(4):
        send(dqg.at[there, :, :, other], dqm.at[there], qc_s.at[there], qc_r.at[there], mate)
        send(gk.at[there], gkm.at[there], pc_s.at[there], pc_r.at[there], mate)
    for there in range(4):
        receive(dqm.at[there], qc_r.at[there], qc_s.at[there])
        receive(gkm.at[there], pc_r.at[there], pc_s.at[there])
    for d in (0, 1, 3, 2):
        there = lax.rem(y + 4 - d, 4)
        receive(xg.at[there, :, 1 - k], xc_r.at[d], xc_s.at[d])
    accq[...] = jnp.zeros_like(accq)
    acck[...] = jnp.zeros_like(acck)

    def weight_step(b, _):
        here = xg[b, :, k].reshape(4 * HALF, 512)
        accq[...] += dot_first(here, dqg[b, :, :, mine].reshape(4 * HALF, 256))
        acck[...] += dot_first(gk[b].reshape(4 * HALF, 128), here)
        here = xg[b, :, 1 - k].reshape(4 * HALF, 512)
        accq[...] += dot_first(here, dqm[b].reshape(4 * HALF, 256))
        acck[...] += dot_first(gkm[b].reshape(4 * HALF, 128), here)
        return 0

    def weight_part(first, last):
        lax.fori_loop(first, last, weight_step, 0)

    weight_part(0, 1)
    for c in range(4):
        for d in (1, 3, 2):
            receive(gyr.at[c, d], gy_r.at[c * 4 + d], gy_s.at[c * 4 + d])
        if c < 2:
            input_send(c + 2)
        gys[c] = (
            gi[c, y].astype(F32)
            + gyr[c, 1].astype(F32)
            + gyr[c, 2].astype(F32)
            + gyr[c, 3].astype(F32)
        ).astype(BF)
        for d in (2, 1, 3):
            send(
                gys.at[c, lax.rem(zh + d, 4)], gzr.at[c, d],
                gz_s.at[c * 4 + d], gz_r.at[c * 4 + d], at_zh(d),
            )
        if c < 3:
            weight_part(1 + c, 2 + c)
    gwq_ref[...] = accq[...]
    gwk_ref[...] = acck[pl.ds(pl.multiple_of(k * 64, 64), 32), :]
    gwv_ref[...] = acck[pl.ds(pl.multiple_of(k * 64 + 32, 32), 32), :]
    for c in range(4):
        for d in (1, 3, 2):
            receive(gzr.at[c, d], gz_r.at[c * 4 + d], gz_s.at[c * 4 + d])
        gi_ref[:, c * 128 : (c + 1) * 128] = (
            gys[c, zh].astype(F32)
            + gzr[c, 1].astype(F32)
            + gzr[c, 2].astype(F32)
            + gzr[c, 3].astype(F32)
        ).astype(BF)
    for copy in pending:
        copy.wait_send()


def write_out(a, b, c, d, a_out, b_out, c_out, d_out, a_tmp, b_tmp, c_tmp, d_tmp, sems):
    ins, temps, outs = (a, b, c, d), (a_tmp, b_tmp, c_tmp, d_tmp), (a_out, b_out, c_out, d_out)
    reads = [pltpu.make_async_copy(ins[i], temps[i], sems.at[0, i]) for i in range(4)]
    writes = [pltpu.make_async_copy(temps[i], outs[i], sems.at[1, i]) for i in range(4)]
    for read in reads:
        read.start()
    for read, write in zip(reads, writes):
        read.wait()
        write.start()
    for write in writes:
        write.wait()


def shards(
    layer_input, w_query, w_key, w_value, query, key, value, context_gradient, positions, segments
):
    vmem = pl.BlockSpec(memory_space=pltpu.VMEM)
    b = lambda *shape: pltpu.VMEM(shape, BF)
    f = lambda *shape: pltpu.VMEM(shape, F32)
    scratch = [
        b(512, 256), b(32, 512), b(32, 512), b(TOK, 256), b(32, TOK), b(32, TOK), b(TOK, 256),
        pltpu.VMEM((1, TOK), jnp.int32), pltpu.VMEM((1, TOK), jnp.int32),
        b(2, 4, 8, HALF, 128), b(4, 4, 16, 256), f(4, TOK, 64), f(4, TOK, 64), b(256, 256),
        b(16, TOK, 128), b(16, TOK, 128), f(16, TOK, LANES), f(16, TOK, LANES), b(4, TOK, LANES),
        b(128, LANES), b(128, LANES), b(LANES, 128), b(LANES, 128),
        b(512, 512), b(128, 512), f(128, LANES),
        b(2, 4, 4, 2, HALF, 128), b(4, 4, 2, HALF, 128), b(4, 4, 2, HALF, 128),
        b(4, 4, 2, HALF, 128), b(4, 2, HALF, 128), b(8, HALF, 128),
        b(4, 4, HALF, 128), b(4, 4, HALF, 128),
        b(2, HALF, 256), b(4, 4, HALF, 512), b(4, 4, HALF, 256), b(4, 4, 2, HALF, 512),
        b(4, 4, 4, HALF, 128), b(4, 4, 4, HALF, 128), b(4, 4, HALF, 128), b(4, 4, HALF, 128),
        f(512, 256), f(128, 512), pltpu.SemaphoreType.DMA((10,)),
    ]
    sizes = [4, 4, 8, 32, 4, 2, 4, 4, 4, 4, 8, 16, 4, 16, 4, 1, 4, 16, 4, 16, 16]
    for size in sizes:
        scratch += [pltpu.SemaphoreType.DMA((size,)), pltpu.SemaphoreType.DMA((size,))]
    gi, gwq, gwk, gwv = pl.pallas_call(
        kernel,
        out_shape=(
            jax.ShapeDtypeStruct((HALF, 512), BF),
            jax.ShapeDtypeStruct((512, 256), F32),
            jax.ShapeDtypeStruct((32, 512), F32),
            jax.ShapeDtypeStruct((32, 512), F32),
        ),
        in_specs=[pl.BlockSpec(memory_space=pl.ANY)] * 10,
        out_specs=(vmem,) * 4,
        scratch_shapes=scratch,
        compiler_params=pltpu.CompilerParams(
            collective_id=0, has_side_effects=True, vmem_limit_bytes=VMEM_BYTES
        ),
        name="attention_backward",
    )(
        layer_input, w_query, w_key.T, w_value.T, query, key.T, value.T, context_gradient,
        positions.reshape(1, TOK), segments.reshape(1, TOK),
    )
    results = (gi, gwq, gwk, gwv)
    anywhere = pl.BlockSpec(memory_space=pl.ANY)
    gi, gwq, gwk, gwv = pl.pallas_call(
        write_out,
        out_shape=tuple(jax.ShapeDtypeStruct(r.shape, r.dtype) for r in results),
        in_specs=[anywhere] * 4,
        out_specs=(anywhere,) * 4,
        scratch_shapes=[pltpu.VMEM(r.shape, r.dtype) for r in results]
        + [pltpu.SemaphoreType.DMA((2, 4))],
        compiler_params=pltpu.CompilerParams(vmem_limit_bytes=VMEM_BYTES),
        name="write_out",
    )(*results)
    return gi, gwq, gwk.T, gwv.T


def solution(mesh):
    return jax.shard_map(
        shards,
        mesh=mesh,
        in_specs=(P("col", "row"),) + (P("row", "col"),) * 7 + (P("row"),) * 2,
        out_specs=(P("col", "row"), P("row", "col"), P("row", "col"), P("row", "col")),
        check_vma=False,
    )
```

```python
import math

import jax
import jax.numpy as jnp
from jax import lax
from jax.experimental import pallas as pl
from jax.experimental.pallas import tpu as pltpu
from jax.sharding import PartitionSpec as P

MESH = pl.DeviceIdType.MESH
BF = jnp.bfloat16
F32 = jnp.float32
HEAD = 128
TOK = 160
HALF = 80
LANES = 384
ROPE_BASE = 500000.0
VMEM_BYTES = 127 * 2**19
SCALE = HEAD ** (-0.5)
RUN = (4, 5, 3, 6, 2, 7, 1)
ROWS = (pl.ds(0, 48), pl.ds(48, 32))


def dot(a, b):
    return lax.dot_general(a, b, (((1,), (0,)), ((), ())), preferred_element_type=F32)


def dot_first(a, b):
    return lax.dot_general(a, b, (((0,), (0,)), ((), ())), preferred_element_type=F32)


def unrotate(gradient, cosines, sines):
    return gradient * cosines + pltpu.roll(gradient, HEAD // 2, 1) * sines


def kernel(
    x_hbm, wq_hbm, wk_hbm, wv_hbm, q_hbm, k_hbm, v_hbm, o_hbm, pos_hbm, seg_hbm,
    gi_ref, gwq_ref, gwk_ref, gwv_ref,
    wq_ref, wk_ref, wv_ref, q_ref, k_ref, v_ref, o_ref, pos_ref, seg_ref,
    kv, meta, cosine, sine, perm, kf, vf, sc, dw, ds, low, qt, ot, qr, orow, wqt, wkv, dqacc,
    dkp, dkr, t1, xr, t2, zr, gk, gkm, dqo, dqg, dqm, xg, gi, gyr, gys, gzr, accq, acck,
    load, mz_s, mz_r, mx_s, mx_r, kz_s, kz_r, kx_s, kx_r, kc_s, kc_r, w_s, w_r,
    xz_s, xz_r, xy_s, xy_r, xc_s, xc_r,
    dc_s, dc_r, dx_s, dx_r, dz_s, dz_r, pz_s, pz_r, px_s, px_r, pc_s, pc_r,
    qm_s, qm_r, qz_s, qz_r, qx_s, qx_r, q2_s, q2_r, qc_s, qc_r, gy_s, gy_r, gz_s, gz_r,
):
    row, col = lax.axis_index("row"), lax.axis_index("col")
    x, zl = lax.div(row, 4), lax.rem(row, 4)
    y, zh, k = lax.div(col, 8), lax.rem(lax.div(col, 2), 4), lax.rem(col, 2)
    pair, h = lax.div(zh, 2), lax.rem(zh, 2)
    w = h * 4 + zl

    def device(x_=x, zl_=zl, y_=y, zh_=zh, k_=k):
        return (x_ * 4 + zl_, y_ * 8 + zh_ * 2 + k_)

    def at_x(d):
        return device(x_=lax.rem(x + d, 4))

    def at_y(d):
        return device(y_=lax.rem(y + d, 4))

    def at_zh(d):
        return device(zh_=lax.rem(zh + d, 4))

    def at_zl(d):
        return device(zl_=lax.rem(zl + d, 4))

    def at_run(e):
        there = lax.rem(w + e, 8)
        return device(zl_=lax.rem(there, 4), zh_=pair * 2 + lax.div(there, 4))

    mate = device(k_=1 - k)
    across = device(zh_=pair * 2 + 1 - h)
    far = [device(zh_=(1 - pair) * 2 + i) for i in range(2)]

    pending = []

    def send(src, dst, s_sem, r_sem, to):
        copy = pltpu.make_async_remote_copy(
            src_ref=src, dst_ref=dst, send_sem=s_sem, recv_sem=r_sem,
            device_id=to, device_id_type=MESH,
        )
        copy.start()
        pending.append(copy)
        return copy

    def receive(dst, r_sem, s_sem):
        pltpu.make_async_remote_copy(
            src_ref=dst, dst_ref=dst, send_sem=s_sem, recv_sem=r_sem,
            device_id=mate, device_id_type=MESH,
        ).wait_recv()

    barrier = pltpu.get_barrier_semaphore()
    peers = [mate] + far
    peers += [at_x(d) for d in (1, 2, 3)] + [at_y(d) for d in (1, 2, 3)]
    peers += [at_run(e) for e in range(1, 8)]
    for peer in peers:
        pl.semaphore_signal(barrier, inc=1, device_id=peer, device_id_type=MESH)

    loads = [
        pltpu.make_async_copy(src, dst, load.at[i])
        for i, (src, dst) in enumerate([
            (k_hbm, k_ref), (v_hbm, v_ref), (pos_hbm, pos_ref), (seg_hbm, seg_ref),
            (x_hbm, xg.at[y, zh, k]), (wk_hbm, wk_ref), (wv_hbm, wv_ref), (wq_hbm, wq_ref),
            (q_hbm, q_ref), (o_hbm, o_ref),
        ])
    ]
    for copy in loads:
        copy.start()
    for copy in loads[:4]:
        copy.wait()

    both = jnp.concatenate([k_ref[...], v_ref[...]], axis=0).astype(F32).T
    kv[k, x, w] = jnp.concatenate([both[:HALF], both[HALF:]], axis=1).astype(BF)
    first_count = jnp.sum(jnp.where(seg_ref[...] == 0, 1.0, 0.0), axis=1, keepdims=True)
    high = lax.div(pos_ref[...], 64)
    rest = pos_ref[...] - high * 64
    line = lax.broadcasted_iota(jnp.int32, (16, TOK), 0)
    facts = jnp.where(line == 0, first_count, jnp.where(line == 1, high.astype(F32), rest.astype(F32)))
    meta[x, zl, :, 0:TOK] = facts.astype(BF)
    meta[x, zl, :, TOK:256] = jnp.zeros((16, 256 - TOK), BF)

    pl.semaphore_wait(barrier, len(peers))

    block = kv.at[k, x, w]
    for d in (2, 1, 3):
        send(block, block, kz_s.at[d], kz_r.at[d], at_zl(d))
    send(block, block, kz_s.at[4], kz_r.at[4], across)
    block = meta.at[x, zl]
    for d in (2, 1, 3):
        send(block, block, mz_s.at[d], mz_r.at[d], at_zl(d))
    block = kv.at[k, x, w]
    for d in (1, 3):
        send(block, block, kx_s.at[d * 8], kx_r.at[d * 8], at_x(d))

    for copy in loads[4:]:
        copy.wait()
    for i in range(2):
        qr[i * TOK : (i + 1) * TOK] = q_ref[:, i * 128 : (i + 1) * 128]
        orow[i * TOK : (i + 1) * TOK] = o_ref[:, i * 128 : (i + 1) * 128]
    qr[2 * TOK : LANES] = jnp.zeros((LANES - 2 * TOK, 128), BF)
    orow[2 * TOK : LANES] = jnp.zeros((LANES - 2 * TOK, 128), BF)
    qt[...] = qr[...].astype(F32).T.astype(BF)
    ot[...] = orow[...].astype(F32).T.astype(BF)

    def run_block(e):
        if e < 4:
            return kv.at[k, x, h * 4 + lax.rem(zl + 4 - e, 4)]
        return kv.at[k, x, (1 - h) * 4 + lax.rem(zl + 8 - e, 4)]

    for e in (1, 3, 2, 4):
        block = run_block(e)
        receive(block, kz_r.at[e], kz_s.at[e])
        if e == 4:
            for d in (2, 1, 3):
                send(block, block, kz_s.at[4 + d], kz_r.at[4 + d], at_zl(d))
        for d in (1, 3):
            send(block, block, kx_s.at[d * 8 + e], kx_r.at[d * 8 + e], at_x(d))
    for d in (1, 3, 2):
        receive(meta.at[x, lax.rem(zl + 4 - d, 4)], mz_r.at[d], mz_s.at[d])
    for d in (1, 3, 2):
        send(meta.at[x], meta.at[x], mx_s.at[d], mx_r.at[d], at_x(d))
    for e in (5, 7, 6):
        block = run_block(e)
        receive(block, kz_r.at[e], kz_s.at[e])
        for d in (1, 3):
            send(block, block, kx_s.at[d * 8 + e], kx_r.at[d * 8 + e], at_x(d))
    send(kv.at[k, x], kv.at[k, x], kx_s.at[16], kx_r.at[16], at_x(2))
    send(kv.at[k, x], kv.at[k, x], kc_s.at[0], kc_r.at[0], mate)
    block = xg.at[y, zh, k]
    for d in (2, 1, 3):
        send(block, block, xz_s.at[d], xz_r.at[d], at_zh(d))

    source = lax.broadcasted_iota(jnp.int32, (256, 256), 0)
    target = lax.broadcasted_iota(jnp.int32, (256, 256), 1)
    wanted = lax.rem(lax.div(target, 32), 2) * 128 + lax.div(target, 64) * 32 + lax.rem(target, 32)
    perm[...] = jnp.where(source == wanted, 1.0, 0.0).astype(BF)
    for d in (1, 3, 2):
        receive(meta.at[lax.rem(x + 4 - d, 4)], mx_r.at[d], mx_s.at[d])
    cut = jnp.zeros((1, 1), F32)
    for xx in range(4):
        for zz in range(4):
            cut = cut + meta[xx, zz].astype(F32)[0:1, 0:1]
    lane = lax.broadcasted_iota(jnp.int32, (1, LANES), 1)
    query = lane - TOK * (lane >= TOK).astype(jnp.int32) - TOK * (lane >= 2 * TOK).astype(jnp.int32)
    query = query + row * TOK
    cut = jnp.broadcast_to(cut, (1, LANES)).astype(jnp.int32)
    begin = jnp.where(query < cut, 0, cut)

    def products(there, peak):
        def step(i, peak):
            at = there * 4 + i
            for half in range(2):
                parts = [kv[kk, there, hh * 4 + i] for hh in range(2) for kk in range(2)]
                lo = 64 * half
                kf[at, half * HALF : (half + 1) * HALF, :] = jnp.concatenate(
                    [p[:, lo : lo + 32] for p in parts], axis=1
                )
                vf[at, half * HALF : (half + 1) * HALF, :] = jnp.concatenate(
                    [p[:, lo + 32 : lo + 64] for p in parts], axis=1
                )
            dw[at] = dot(vf[at], ot[...])
            key = at * TOK + lax.broadcasted_iota(jnp.int32, (TOK, LANES), 0)
            seen = (key >= begin) & (key <= query)
            seen = jnp.where(seen, dot(kf[at], qt[...]) * SCALE, -1e30)
            sc[at] = seen
            return jnp.maximum(peak, jnp.max(seen, axis=0, keepdims=True))

        return lax.fori_loop(0, 4, step, peak, unroll=2)

    receive(kv.at[1 - k, x], kc_r.at[0], kc_s.at[0])
    peak = products(x, jnp.full((1, LANES), -1e30, F32))
    place = lax.broadcasted_iota(jnp.int32, (HEAD, TOK), 0)
    freq = jnp.exp(-(2.0 * lax.rem(place, 64).astype(F32) / HEAD) * math.log(ROPE_BASE))
    sign = jnp.where(place < 64, 1.0, -1.0)

    def tables(i, _):
        facts = meta[x, i].astype(F32)
        angle = (facts[1:2, 0:TOK] * 64.0 + facts[2:3, 0:TOK]) * freq
        cosine[i] = jnp.cos(angle).T
        sine[i] = (jnp.sin(angle) * sign).T
        return 0

    lax.fori_loop(0, 4, tables, 0)
    def pass_on(d):
        there = lax.rem(x + 4 - d, 4)
        if d == 2:
            receive(kv.at[k, there], kx_r.at[16], kx_s.at[16])
        else:
            for e in range(8):
                near = h * 4 + lax.rem(zl + 4 - e, 4)
                at = near if e < 4 else (1 - h) * 4 + lax.rem(zl + 8 - e, 4)
                receive(kv.at[k, there, at], kx_r.at[d * 8 + e], kx_s.at[d * 8 + e])
        send(kv.at[k, there], kv.at[k, there], kc_s.at[d], kc_r.at[d], mate)

    pass_on(1)
    pass_on(3)
    for d in (1, 3, 2):
        there = lax.rem(x + 4 - d, 4)
        receive(kv.at[1 - k, there], kc_r.at[d], kc_s.at[d])
        peak = products(there, peak)
        if d == 1:
            pass_on(2)


    def sum_step(b, sums):
        total, delta = sums
        term = jnp.exp(sc[b] - peak)
        sc[b] = term
        return (
            total + jnp.sum(term, axis=0, keepdims=True),
            delta + jnp.sum(term * dw[b], axis=0, keepdims=True),
        )

    zero = jnp.zeros((1, LANES), F32)
    total, delta = lax.fori_loop(0, 16, sum_step, (zero, zero))
    inverse = 1.0 / total
    delta = delta * inverse

    dqacc[...] = jnp.zeros_like(dqacc)
    cosines, sines = cosine[zl], sine[zl]

    def key_send(d, part):
        there, rows = lax.rem(x + d, 4), ROWS[part]
        send(
            t1.at[there, :, :, rows], xr.at[d, :, :, rows],
            dx_s.at[d * 2 + part], dx_r.at[d * 2 + part], at_x(d),
        )

    def key_sum(d):
        there = lax.rem(x + d, 4)
        receive(dkr.at[there], dc_r.at[d], dc_s.at[d])
        t1[there] = (dkp[k, there].astype(F32) + dkr[there].astype(F32)).astype(BF)
        if d:
            key_send(d, 0)

    def score_grads(there, _):
        for i in range(4):
            b = there * 4 + i
            weights = sc[b] * inverse
            ds[b] = (weights * (dw[b] - delta) * SCALE).astype(BF)
            low[b] = weights.astype(BF)
        dqacc[...] += dot_first(
            kf[pl.ds(there * 4, 4)].reshape(4 * TOK, HEAD),
            ds[pl.ds(there * 4, 4)].reshape(4 * TOK, LANES),
        )
        return 0

    lax.fori_loop(0, 4, score_grads, 0)
    dquery = dqacc[...].T
    for head in range(2):
        part = dquery[head * TOK : (head + 1) * TOK]
        both = unrotate(part, cosines, sines).astype(BF)
        for half in range(2):
            dqo[half, :, head * 128 : (head + 1) * 128] = both[half * HALF : (half + 1) * HALF]
    mine = pl.ds(pl.multiple_of(k * 256, 256), 256)
    other = pl.ds(pl.multiple_of((1 - k) * 256, 256), 256)
    send(dqo.at[1 - k], dqg.at[x, zl, :, mine], qm_s.at[0], qm_r.at[0], mate)
    dqg[x, zl, :, mine] = dqo[k]

    before = None
    for d in (2, 1, 3, 0):
        there = lax.rem(x + d, 4)

        def grad_step(i, _):
            b = there * 4 + i
            dkey = dot(ds[b], qr[...]).astype(BF)
            dvalue = dot(low[b], orow[...]).astype(BF)
            for half in range(2):
                dkp[half, there, i, 0] = dkey[half * HALF : (half + 1) * HALF]
                dkp[half, there, i, 1] = dvalue[half * HALF : (half + 1) * HALF]
            return 0

        lax.fori_loop(0, 4, grad_step, 0, unroll=2)
        send(dkp.at[1 - k, there], dkr.at[there], dc_s.at[d], dc_r.at[d], mate)
        if before is None:
            receive(dqg.at[x, zl, :, other], qm_r.at[0], qm_s.at[0])
            block = dqg.at[x, zl]
            for e in (2, 1, 3):
                send(block, block, qz_s.at[e], qz_r.at[e], at_zl(e))
        else:
            key_sum(before)
        before = d
    key_sum(0)
    for d in (2, 1, 3):
        key_send(d, 1)
    block = dqg.at[x, zl]
    for d in (1, 3):
        send(block, block, qx_s.at[d * 4], qx_r.at[d * 4], at_x(d))

    rows = pl.ds(pl.multiple_of(k * 64, 64), 64)
    wkv[rows, :] = jnp.concatenate([wk_ref[...], wv_ref[...]], axis=0)
    send(wkv.at[rows], wkv.at[rows], w_s.at[1], w_r.at[1], mate)
    rows = pl.ds(pl.multiple_of(k * 256, 256), 256)
    wqt[rows, :] = wq_ref[...].astype(F32).T.astype(BF)
    send(wqt.at[rows], wqt.at[rows], w_s.at[0], w_r.at[0], mate)
    for d in (1, 3, 2):
        receive(xg.at[y, lax.rem(zh + 4 - d, 4), k], xz_r.at[d], xz_s.at[d])
    block = xg.at[y, :, k]
    for d in (2, 1, 3):
        send(block, block, xy_s.at[d], xy_r.at[d], at_y(d))
    send(block, block, xc_s.at[0], xc_r.at[0], mate)

    def x_sum(part):
        lo, size = (0, 48) if part == 0 else (48, 32)
        at = pl.ds(pl.multiple_of(k * HALF + lo, 16), size)

        def step(i, _):
            total = t1[x, i, :, lo : lo + size].astype(F32)
            for d in range(1, 4):
                total = total + xr[d, i, :, lo : lo + size].astype(F32)
            turned = unrotate(total[0], cosine[i, at, :], sine[i, at, :])
            wide = jnp.concatenate([turned, total[1]], axis=1).astype(BF)
            wide = dot(wide, perm[...]).astype(BF)
            t2[i, 0, lo : lo + size] = wide[:, :128]
            t2[i, 1, lo : lo + size] = wide[:, 128:]
            return 0

        lax.fori_loop(0, 4, step, 0, unroll=True)

    for part in range(2):
        for d in (1, 3, 2):
            rows = ROWS[part]
            receive(xr.at[d, :, :, rows], dx_r.at[d * 2 + part], dx_s.at[d * 2 + part])
        x_sum(part)
        for e in RUN:
            to = lax.rem(w + e, 8)
            send(
                t2.at[lax.rem(to, 4), lax.div(to, 4), rows], zr.at[e, rows],
                dz_s.at[e * 2 + part], dz_r.at[e * 2 + part], at_run(e),
            )

    for e in (1, 3, 2):
        block = dqg.at[x, lax.rem(zl + 4 - e, 4)]
        receive(block, qz_r.at[e], qz_s.at[e])
        for d in (1, 3):
            send(block, block, qx_s.at[d * 4 + e], qx_r.at[d * 4 + e], at_x(d))

    def relay(e):
        for part, d in enumerate((1, 3)):
            block = dqg.at[lax.rem(x + 4 - d, 4), lax.rem(zl + 4 - e, 4)]
            receive(block, qx_r.at[d * 4 + e], qx_s.at[d * 4 + e])
            block = block.at[:, pl.ds(part * 256, 256)]
            send(block, block, q2_s.at[part * 4 + e], q2_r.at[part * 4 + e], at_x(d))

    relay(0)

    for part in range(2):
        for e in RUN:
            rows = ROWS[part]
            receive(zr.at[e, rows], dz_r.at[e * 2 + part], dz_s.at[e * 2 + part])
    summed = t2[zl, h].astype(F32)
    for e in range(1, 8):
        summed = summed + zr[e].astype(F32)
    gk[x, zl] = summed.astype(BF)
    block = gk.at[x, zl]
    for d in (2, 1, 3):
        send(block, block, pz_s.at[d], pz_r.at[d], at_zl(d))
    for d in (2, 1, 3):
        send(block, block, px_s.at[d * 4], px_r.at[d * 4], at_x(d))
    for e in (1, 3, 2):
        relay(e)
    for e in (1, 3, 2):
        block = gk.at[x, lax.rem(zl + 4 - e, 4)]
        receive(block, pz_r.at[e], pz_s.at[e])
        for d in (2, 1, 3):
            send(block, block, px_s.at[d * 4 + e], px_r.at[d * 4 + e], at_x(d))
    for d in (1, 3, 2):
        there = lax.rem(y + 4 - d, 4)
        block = xg.at[there, :, k]
        receive(block, xy_r.at[d], xy_s.at[d])
        send(block, block, xc_s.at[d], xc_r.at[d], mate)

    receive(wqt.at[pl.ds(pl.multiple_of((1 - k) * 256, 256), 256)], w_r.at[0], w_s.at[0])
    receive(wkv.at[pl.ds(pl.multiple_of((1 - k) * 64, 64), 64)], w_r.at[1], w_s.at[1])
    for e in range(4):
        for part in range(2):
            block = dqg.at[lax.rem(x + 2, 4), lax.rem(zl + 4 - e, 4), :, pl.ds(part * 256, 256)]
            receive(block, q2_r.at[part * 4 + e], q2_s.at[part * 4 + e])
    for d in (1, 3, 2):
        there = lax.rem(x + 4 - d, 4)
        for e in range(4):
            block = gk.at[there, lax.rem(zl + 4 - e, 4)]
            receive(block, px_r.at[d * 4 + e], px_s.at[d * 4 + e])

    def input_part(c):
        rows = slice(c * 16, (c + 1) * 16)
        gi[c] = (
            (
                dot(dqg[:, :, rows, :].reshape(256, 512), wqt[...])
                + dot(gk[:, :, rows, :].reshape(256, 128), wkv[...])
            )
            .astype(BF)
            .reshape(4, 4, 16, 512)
        )

    def input_send(c):
        return [
            send(
                gi.at[c, lax.rem(y + d, 4)], gyr.at[c, d],
                gy_s.at[c * 4 + d], gy_r.at[c * 4 + d], at_y(d),
            )
            for d in (2, 1, 3)
        ]

    def sent(copies):
        for copy in copies:
            copy.wait_send()
            pending[:] = [other for other in pending if other is not copy]

    def input_sum(c):
        for d in (1, 3, 2):
            receive(gyr.at[c, d], gy_r.at[c * 4 + d], gy_s.at[c * 4 + d])
        gys[c] = (
            gi[c, y].astype(F32)
            + gyr[c, 1].astype(F32)
            + gyr[c, 2].astype(F32)
            + gyr[c, 3].astype(F32)
        ).astype(BF)
        for d in (2, 1, 3):
            send(
                gys.at[c, lax.rem(zh + d, 4)], gzr.at[c, d],
                gz_s.at[c * 4 + d], gz_r.at[c * 4 + d], at_zh(d),
            )

    flying = []
    for c in range(5):
        input_part(c)
        if c == 4:
            input_sum(0)
        if c >= 2:
            sent(flying[c - 2])
        flying.append(input_send(c))

    for there in range(4):
        send(dqg.at[there, :, :, other], dqm.at[there], qc_s.at[there], qc_r.at[there], mate)
        send(gk.at[there], gkm.at[there], pc_s.at[there], pc_r.at[there], mate)
    for there in range(4):
        receive(dqm.at[there], qc_r.at[there], qc_s.at[there])
        receive(gkm.at[there], pc_r.at[there], pc_s.at[there])
    for d in (0, 1, 3, 2):
        there = lax.rem(y + 4 - d, 4)
        receive(xg.at[there, :, 1 - k], xc_r.at[d], xc_s.at[d])
    accq[...] = jnp.zeros_like(accq)
    acck[...] = jnp.zeros_like(acck)

    def weight_step(b, _):
        here = xg[b, :, k].reshape(4 * HALF, 512)
        accq[...] += dot_first(here, dqg[b, :, :, mine].reshape(4 * HALF, 256))
        acck[...] += dot_first(gk[b].reshape(4 * HALF, 128), here)
        here = xg[b, :, 1 - k].reshape(4 * HALF, 512)
        accq[...] += dot_first(here, dqm[b].reshape(4 * HALF, 256))
        acck[...] += dot_first(gkm[b].reshape(4 * HALF, 128), here)
        return 0

    def weight_part(first, last):
        lax.fori_loop(first, last, weight_step, 0)

    weight_part(0, 1)
    for c in range(1, 5):
        input_sum(c)
        if c < 4:
            weight_part(c, c + 1)
    gwq_ref[...] = accq[...]
    gwk_ref[...] = acck[pl.ds(pl.multiple_of(k * 64, 64), 32), :]
    gwv_ref[...] = acck[pl.ds(pl.multiple_of(k * 64 + 32, 32), 32), :]
    for c in range(5):
        for d in (1, 3, 2):
            receive(gzr.at[c, d], gz_r.at[c * 4 + d], gz_s.at[c * 4 + d])
        gi_ref[c * 16 : (c + 1) * 16, :] = (
            gys[c, zh].astype(F32)
            + gzr[c, 1].astype(F32)
            + gzr[c, 2].astype(F32)
            + gzr[c, 3].astype(F32)
        ).astype(BF)
    for copy in pending:
        copy.wait_send()


def write_out(a, b, c, d, a_out, b_out, c_out, d_out, a_tmp, b_tmp, c_tmp, d_tmp, sems):
    ins, temps, outs = (a, b, c, d), (a_tmp, b_tmp, c_tmp, d_tmp), (a_out, b_out, c_out, d_out)
    reads = [pltpu.make_async_copy(ins[i], temps[i], sems.at[0, i]) for i in range(4)]
    writes = [pltpu.make_async_copy(temps[i], outs[i], sems.at[1, i]) for i in range(4)]
    for read in reads:
        read.start()
    for read, write in zip(reads, writes):
        read.wait()
        write.start()
    for write in writes:
        write.wait()


def shards(
    layer_input, w_query, w_key, w_value, query, key, value, context_gradient, positions, segments
):
    vmem = pl.BlockSpec(memory_space=pltpu.VMEM)
    b = lambda *shape: pltpu.VMEM(shape, BF)
    f = lambda *shape: pltpu.VMEM(shape, F32)
    scratch = [
        b(512, 256), b(32, 512), b(32, 512), b(TOK, 256), b(32, TOK), b(32, TOK), b(TOK, 256),
        pltpu.VMEM((1, TOK), jnp.int32), pltpu.VMEM((1, TOK), jnp.int32),
        b(2, 4, 8, HALF, 128), b(4, 4, 16, 256), f(4, TOK, HEAD), f(4, TOK, HEAD), b(256, 256),
        b(16, TOK, 128), b(16, TOK, 128), f(16, TOK, LANES), f(16, TOK, LANES), b(16, TOK, LANES), b(16, TOK, LANES),
        b(128, LANES), b(128, LANES), b(LANES, 128), b(LANES, 128),
        b(512, 512), b(128, 512), f(128, LANES),
        b(2, 4, 4, 2, HALF, 128), b(4, 4, 2, HALF, 128), b(4, 4, 2, HALF, 128),
        b(4, 4, 2, HALF, 128), b(4, 2, HALF, 128), b(8, HALF, 128),
        b(4, 4, HALF, 128), b(4, 4, HALF, 128),
        b(2, HALF, 256), b(4, 4, HALF, 512), b(4, 4, HALF, 256), b(4, 4, 2, HALF, 512),
        b(5, 4, 4, 16, 512), b(5, 4, 4, 16, 512), b(5, 4, 16, 512), b(5, 4, 16, 512),
        f(512, 256), f(128, 512), pltpu.SemaphoreType.DMA((10,)),
    ]
    sizes = [4, 4, 8, 32, 4, 2, 4, 4, 4, 4, 8, 16, 4, 16, 4, 1, 4, 16, 8, 4, 20, 20]
    for size in sizes:
        scratch += [pltpu.SemaphoreType.DMA((size,)), pltpu.SemaphoreType.DMA((size,))]
    gi, gwq, gwk, gwv = pl.pallas_call(
        kernel,
        out_shape=(
            jax.ShapeDtypeStruct((HALF, 512), BF),
            jax.ShapeDtypeStruct((512, 256), F32),
            jax.ShapeDtypeStruct((32, 512), F32),
            jax.ShapeDtypeStruct((32, 512), F32),
        ),
        in_specs=[pl.BlockSpec(memory_space=pl.ANY)] * 10,
        out_specs=(vmem,) * 4,
        scratch_shapes=scratch,
        compiler_params=pltpu.CompilerParams(
            collective_id=0, has_side_effects=True, vmem_limit_bytes=VMEM_BYTES
        ),
        name="attention_backward",
    )(
        layer_input, w_query, w_key.T, w_value.T, query, key.T, value.T, context_gradient,
        positions.reshape(1, TOK), segments.reshape(1, TOK),
    )
    results = (gi, gwq, gwk, gwv)
    anywhere = pl.BlockSpec(memory_space=pl.ANY)
    gi, gwq, gwk, gwv = pl.pallas_call(
        write_out,
        out_shape=tuple(jax.ShapeDtypeStruct(r.shape, r.dtype) for r in results),
        in_specs=[anywhere] * 4,
        out_specs=(anywhere,) * 4,
        scratch_shapes=[pltpu.VMEM(r.shape, r.dtype) for r in results]
        + [pltpu.SemaphoreType.DMA((2, 4))],
        compiler_params=pltpu.CompilerParams(vmem_limit_bytes=VMEM_BYTES),
        name="write_out",
    )(*results)
    return gi, gwq, gwk.T, gwv.T


def solution(mesh):
    return jax.shard_map(
        shards,
        mesh=mesh,
        in_specs=(P("col", "row"),) + (P("row", "col"),) * 7 + (P("row"),) * 2,
        out_specs=(P("col", "row"), P("row", "col"), P("row", "col"), P("row", "col")),
        check_vma=False,
    )
```

```python
import math

import jax
import jax.numpy as jnp
from jax import lax
from jax.experimental import pallas as pl
from jax.experimental.pallas import tpu as pltpu
from jax.sharding import PartitionSpec as P

MESH = pl.DeviceIdType.MESH
BF = jnp.bfloat16
F32 = jnp.float32
HEAD = 128
TOK = 160
HALF = 80
LANES = 384
ROPE_BASE = 500000.0
VMEM_BYTES = 127 * 2**19
SCALE = HEAD ** (-0.5)
RUN = (4, 5, 3, 6, 2, 7, 1)
ROWS = (pl.ds(0, 48), pl.ds(48, 32))


def dot(a, b):
    return lax.dot_general(a, b, (((1,), (0,)), ((), ())), preferred_element_type=F32)


def dot_first(a, b):
    return lax.dot_general(a, b, (((0,), (0,)), ((), ())), preferred_element_type=F32)


def unrotate(gradient, cosines, sines):
    return gradient * cosines + pltpu.roll(gradient, HEAD // 2, 1) * sines


def kernel(
    x_hbm, wq_hbm, wk_hbm, wv_hbm, q_hbm, k_hbm, v_hbm, o_hbm, pos_hbm, seg_hbm,
    gi_ref, gwq_ref, gwk_ref, gwv_ref,
    wq_ref, wk_ref, wv_ref, q_ref, k_ref, v_ref, o_ref, pos_ref, seg_ref,
    kv, meta, cosine, sine, perm, kf, vf, sc, dw, ds, low, qt, ot, qr, orow, wqt, wkv, dqacc,
    dkp, dkr, t1, xr, t2, zr, gk, gkm, dqo, dqg, dqm, xg, gi, gyr, gys, gzr, accq, acck,
    load, mz_s, mz_r, mx_s, mx_r, kz_s, kz_r, kx_s, kx_r, kc_s, kc_r, w_s, w_r,
    xz_s, xz_r, xy_s, xy_r, xc_s, xc_r,
    dc_s, dc_r, dx_s, dx_r, dz_s, dz_r, pz_s, pz_r, px_s, px_r, pc_s, pc_r,
    qm_s, qm_r, qz_s, qz_r, qx_s, qx_r, q2_s, q2_r, qc_s, qc_r, gy_s, gy_r, gz_s, gz_r,
):
    row, col = lax.axis_index("row"), lax.axis_index("col")
    x, zl = lax.div(row, 4), lax.rem(row, 4)
    y, zh, k = lax.div(col, 8), lax.rem(lax.div(col, 2), 4), lax.rem(col, 2)
    pair, h = lax.div(zh, 2), lax.rem(zh, 2)
    w = h * 4 + zl

    def device(x_=x, zl_=zl, y_=y, zh_=zh, k_=k):
        return (x_ * 4 + zl_, y_ * 8 + zh_ * 2 + k_)

    def at_x(d):
        return device(x_=lax.rem(x + d, 4))

    def at_y(d):
        return device(y_=lax.rem(y + d, 4))

    def at_zh(d):
        return device(zh_=lax.rem(zh + d, 4))

    def at_zl(d):
        return device(zl_=lax.rem(zl + d, 4))

    def at_run(e):
        there = lax.rem(w + e, 8)
        return device(zl_=lax.rem(there, 4), zh_=pair * 2 + lax.div(there, 4))

    mate = device(k_=1 - k)
    across = device(zh_=pair * 2 + 1 - h)
    far = [device(zh_=(1 - pair) * 2 + i) for i in range(2)]

    pending = []

    def send(src, dst, s_sem, r_sem, to):
        copy = pltpu.make_async_remote_copy(
            src_ref=src, dst_ref=dst, send_sem=s_sem, recv_sem=r_sem,
            device_id=to, device_id_type=MESH,
        )
        copy.start()
        pending.append(copy)
        return copy

    def receive(dst, r_sem, s_sem):
        pltpu.make_async_remote_copy(
            src_ref=dst, dst_ref=dst, send_sem=s_sem, recv_sem=r_sem,
            device_id=mate, device_id_type=MESH,
        ).wait_recv()

    barrier = pltpu.get_barrier_semaphore()
    peers = [mate] + far
    peers += [at_x(d) for d in (1, 2, 3)] + [at_y(d) for d in (1, 2, 3)]
    peers += [at_run(e) for e in range(1, 8)]
    for peer in peers:
        pl.semaphore_signal(barrier, inc=1, device_id=peer, device_id_type=MESH)

    loads = [
        pltpu.make_async_copy(src, dst, load.at[i])
        for i, (src, dst) in enumerate([
            (k_hbm, k_ref), (v_hbm, v_ref), (pos_hbm, pos_ref), (seg_hbm, seg_ref),
            (x_hbm, xg.at[y, zh, k]), (wk_hbm, wk_ref), (wv_hbm, wv_ref), (wq_hbm, wq_ref),
            (q_hbm, q_ref), (o_hbm, o_ref),
        ])
    ]
    for copy in loads:
        copy.start()
    for copy in loads[:4]:
        copy.wait()

    both = jnp.concatenate([k_ref[...], v_ref[...]], axis=0).astype(F32).T
    kv[k, x, w] = jnp.concatenate([both[:HALF], both[HALF:]], axis=1).astype(BF)
    first_count = jnp.sum(jnp.where(seg_ref[...] == 0, 1.0, 0.0), axis=1, keepdims=True)
    high = lax.div(pos_ref[...], 64)
    rest = pos_ref[...] - high * 64
    line = lax.broadcasted_iota(jnp.int32, (16, TOK), 0)
    facts = jnp.where(line == 0, first_count, jnp.where(line == 1, high.astype(F32), rest.astype(F32)))
    meta[x, zl, :, 0:TOK] = facts.astype(BF)
    meta[x, zl, :, TOK:256] = jnp.zeros((16, 256 - TOK), BF)

    pl.semaphore_wait(barrier, len(peers))

    block = kv.at[k, x, w]
    for d in (2, 1, 3):
        send(block, block, kz_s.at[d], kz_r.at[d], at_zl(d))
    send(block, block, kz_s.at[4], kz_r.at[4], across)
    block = meta.at[x, zl]
    for d in (2, 1, 3):
        send(block, block, mz_s.at[d], mz_r.at[d], at_zl(d))
    block = kv.at[k, x, w]
    for d in (1, 3):
        send(block, block, kx_s.at[d * 8], kx_r.at[d * 8], at_x(d))

    for copy in loads[4:]:
        copy.wait()
    for i in range(2):
        qr[i * TOK : (i + 1) * TOK] = q_ref[:, i * 128 : (i + 1) * 128]
        orow[i * TOK : (i + 1) * TOK] = o_ref[:, i * 128 : (i + 1) * 128]
    qr[2 * TOK : LANES] = jnp.zeros((LANES - 2 * TOK, 128), BF)
    orow[2 * TOK : LANES] = jnp.zeros((LANES - 2 * TOK, 128), BF)
    qt[...] = qr[...].astype(F32).T.astype(BF)
    ot[...] = orow[...].astype(F32).T.astype(BF)

    def run_block(e):
        if e < 4:
            return kv.at[k, x, h * 4 + lax.rem(zl + 4 - e, 4)]
        return kv.at[k, x, (1 - h) * 4 + lax.rem(zl + 8 - e, 4)]

    for e in (1, 3, 2, 4):
        block = run_block(e)
        receive(block, kz_r.at[e], kz_s.at[e])
        if e == 4:
            for d in (2, 1, 3):
                send(block, block, kz_s.at[4 + d], kz_r.at[4 + d], at_zl(d))
        for d in (1, 3):
            send(block, block, kx_s.at[d * 8 + e], kx_r.at[d * 8 + e], at_x(d))
    for d in (1, 3, 2):
        receive(meta.at[x, lax.rem(zl + 4 - d, 4)], mz_r.at[d], mz_s.at[d])
    for d in (1, 3, 2):
        send(meta.at[x], meta.at[x], mx_s.at[d], mx_r.at[d], at_x(d))
    for e in (5, 7, 6):
        block = run_block(e)
        receive(block, kz_r.at[e], kz_s.at[e])
        for d in (1, 3):
            send(block, block, kx_s.at[d * 8 + e], kx_r.at[d * 8 + e], at_x(d))
    send(kv.at[k, x], kv.at[k, x], kx_s.at[16], kx_r.at[16], at_x(2))
    send(kv.at[k, x], kv.at[k, x], kc_s.at[0], kc_r.at[0], mate)
    block = xg.at[y, zh, k]
    for d in (2, 1, 3):
        send(block, block, xz_s.at[d], xz_r.at[d], at_zh(d))

    source = lax.broadcasted_iota(jnp.int32, (256, 256), 0)
    target = lax.broadcasted_iota(jnp.int32, (256, 256), 1)
    wanted = lax.rem(lax.div(target, 32), 2) * 128 + lax.div(target, 64) * 32 + lax.rem(target, 32)
    perm[...] = jnp.where(source == wanted, 1.0, 0.0).astype(BF)
    for d in (1, 3, 2):
        receive(meta.at[lax.rem(x + 4 - d, 4)], mx_r.at[d], mx_s.at[d])
    cut = jnp.zeros((1, 1), F32)
    for xx in range(4):
        for zz in range(4):
            cut = cut + meta[xx, zz].astype(F32)[0:1, 0:1]
    lane = lax.broadcasted_iota(jnp.int32, (1, LANES), 1)
    query = lane - TOK * (lane >= TOK).astype(jnp.int32) - TOK * (lane >= 2 * TOK).astype(jnp.int32)
    query = query + row * TOK
    cut = jnp.broadcast_to(cut, (1, LANES)).astype(jnp.int32)
    begin = jnp.where(query < cut, 0, cut)

    def products(there, peak):
        def step(i, peak):
            at = there * 4 + i
            for half in range(2):
                parts = [kv[kk, there, hh * 4 + i] for hh in range(2) for kk in range(2)]
                lo = 64 * half
                kf[at, half * HALF : (half + 1) * HALF, :] = jnp.concatenate(
                    [p[:, lo : lo + 32] for p in parts], axis=1
                )
                vf[at, half * HALF : (half + 1) * HALF, :] = jnp.concatenate(
                    [p[:, lo + 32 : lo + 64] for p in parts], axis=1
                )
            dw[at] = dot(vf[at], ot[...])
            key = at * TOK + lax.broadcasted_iota(jnp.int32, (TOK, LANES), 0)
            seen = (key >= begin) & (key <= query)
            seen = jnp.where(seen, dot(kf[at], qt[...]) * SCALE, -1e30)
            sc[at] = seen
            return jnp.maximum(peak, jnp.max(seen, axis=0, keepdims=True))

        return lax.fori_loop(0, 4, step, peak, unroll=2)

    receive(kv.at[1 - k, x], kc_r.at[0], kc_s.at[0])
    peak = products(x, jnp.full((1, LANES), -1e30, F32))
    place = lax.broadcasted_iota(jnp.int32, (HEAD, TOK), 0)
    freq = jnp.exp(-(2.0 * lax.rem(place, 64).astype(F32) / HEAD) * math.log(ROPE_BASE))
    sign = jnp.where(place < 64, 1.0, -1.0)

    def tables(i, _):
        facts = meta[x, i].astype(F32)
        angle = (facts[1:2, 0:TOK] * 64.0 + facts[2:3, 0:TOK]) * freq
        cosine[i] = jnp.cos(angle).T
        sine[i] = (jnp.sin(angle) * sign).T
        return 0

    lax.fori_loop(0, 4, tables, 0)
    def pass_on(d):
        there = lax.rem(x + 4 - d, 4)
        if d == 2:
            receive(kv.at[k, there], kx_r.at[16], kx_s.at[16])
        else:
            for e in range(8):
                near = h * 4 + lax.rem(zl + 4 - e, 4)
                at = near if e < 4 else (1 - h) * 4 + lax.rem(zl + 8 - e, 4)
                receive(kv.at[k, there, at], kx_r.at[d * 8 + e], kx_s.at[d * 8 + e])
        send(kv.at[k, there], kv.at[k, there], kc_s.at[d], kc_r.at[d], mate)

    pass_on(1)
    pass_on(3)
    for d in (1, 3, 2):
        there = lax.rem(x + 4 - d, 4)
        receive(kv.at[1 - k, there], kc_r.at[d], kc_s.at[d])
        peak = products(there, peak)
        if d == 1:
            pass_on(2)


    def sum_step(b, sums):
        total, delta = sums
        term = jnp.exp(sc[b] - peak)
        sc[b] = term
        return (
            total + jnp.sum(term, axis=0, keepdims=True),
            delta + jnp.sum(term * dw[b], axis=0, keepdims=True),
        )

    zero = jnp.zeros((1, LANES), F32)
    total, delta = lax.fori_loop(0, 16, sum_step, (zero, zero))
    inverse = 1.0 / total
    delta = delta * inverse

    dqacc[...] = jnp.zeros_like(dqacc)
    cosines, sines = cosine[zl], sine[zl]

    def key_send(d, part):
        there, rows = lax.rem(x + d, 4), ROWS[part]
        send(
            t1.at[there, :, :, rows], xr.at[d, :, :, rows],
            dx_s.at[d * 2 + part], dx_r.at[d * 2 + part], at_x(d),
        )

    def key_sum(d):
        there = lax.rem(x + d, 4)
        receive(dkr.at[there], dc_r.at[d], dc_s.at[d])
        t1[there] = (dkp[k, there].astype(F32) + dkr[there].astype(F32)).astype(BF)
        if d:
            key_send(d, 0)

    def score_grads(there, _):
        for i in range(4):
            b = there * 4 + i
            weights = sc[b] * inverse
            ds[b] = (weights * (dw[b] - delta) * SCALE).astype(BF)
            low[b] = weights.astype(BF)
        dqacc[...] += dot_first(
            kf[pl.ds(there * 4, 4)].reshape(4 * TOK, HEAD),
            ds[pl.ds(there * 4, 4)].reshape(4 * TOK, LANES),
        )
        return 0

    before = None
    for d in (2, 1, 3, 0):
        there = lax.rem(x + d, 4)
        score_grads(there, 0)

        def grad_step(i, _):
            b = there * 4 + i
            dkey = dot(ds[b], qr[...]).astype(BF)
            dvalue = dot(low[b], orow[...]).astype(BF)
            for half in range(2):
                dkp[half, there, i, 0] = dkey[half * HALF : (half + 1) * HALF]
                dkp[half, there, i, 1] = dvalue[half * HALF : (half + 1) * HALF]
            return 0

        lax.fori_loop(0, 4, grad_step, 0, unroll=2)
        send(dkp.at[1 - k, there], dkr.at[there], dc_s.at[d], dc_r.at[d], mate)
        if before is not None:
            key_sum(before)
        before = d
    dquery = dqacc[...].T
    for head in range(2):
        part = dquery[head * TOK : (head + 1) * TOK]
        both = unrotate(part, cosines, sines).astype(BF)
        for half in range(2):
            dqo[half, :, head * 128 : (head + 1) * 128] = both[half * HALF : (half + 1) * HALF]
    mine = pl.ds(pl.multiple_of(k * 256, 256), 256)
    other = pl.ds(pl.multiple_of((1 - k) * 256, 256), 256)
    send(dqo.at[1 - k], dqg.at[x, zl, :, mine], qm_s.at[0], qm_r.at[0], mate)
    dqg[x, zl, :, mine] = dqo[k]

    key_sum(0)
    for d in (2, 1, 3):
        key_send(d, 1)
    receive(dqg.at[x, zl, :, other], qm_r.at[0], qm_s.at[0])
    block = dqg.at[x, zl]
    for e in (2, 1, 3):
        send(block, block, qz_s.at[e], qz_r.at[e], at_zl(e))

    rows = pl.ds(pl.multiple_of(k * 64, 64), 64)
    wkv[rows, :] = jnp.concatenate([wk_ref[...], wv_ref[...]], axis=0)
    send(wkv.at[rows], wkv.at[rows], w_s.at[1], w_r.at[1], mate)
    rows = pl.ds(pl.multiple_of(k * 256, 256), 256)
    wqt[rows, :] = wq_ref[...].astype(F32).T.astype(BF)
    send(wqt.at[rows], wqt.at[rows], w_s.at[0], w_r.at[0], mate)
    for d in (1, 3, 2):
        receive(xg.at[y, lax.rem(zh + 4 - d, 4), k], xz_r.at[d], xz_s.at[d])
    block = xg.at[y, :, k]
    for d in (2, 1, 3):
        send(block, block, xy_s.at[d], xy_r.at[d], at_y(d))
    send(block, block, xc_s.at[0], xc_r.at[0], mate)

    def x_sum(part):
        lo, size = (0, 48) if part == 0 else (48, 32)
        at = pl.ds(pl.multiple_of(k * HALF + lo, 16), size)

        def step(i, _):
            total = t1[x, i, :, lo : lo + size].astype(F32)
            for d in range(1, 4):
                total = total + xr[d, i, :, lo : lo + size].astype(F32)
            turned = unrotate(total[0], cosine[i, at, :], sine[i, at, :])
            wide = jnp.concatenate([turned, total[1]], axis=1).astype(BF)
            wide = dot(wide, perm[...]).astype(BF)
            t2[i, 0, lo : lo + size] = wide[:, :128]
            t2[i, 1, lo : lo + size] = wide[:, 128:]
            return 0

        lax.fori_loop(0, 4, step, 0, unroll=True)

    for part in range(2):
        for d in (1, 3, 2):
            rows = ROWS[part]
            receive(xr.at[d, :, :, rows], dx_r.at[d * 2 + part], dx_s.at[d * 2 + part])
        x_sum(part)
        for e in RUN:
            to = lax.rem(w + e, 8)
            send(
                t2.at[lax.rem(to, 4), lax.div(to, 4), rows], zr.at[e, rows],
                dz_s.at[e * 2 + part], dz_r.at[e * 2 + part], at_run(e),
            )

    block = dqg.at[x, zl]
    for d in (1, 3):
        send(block, block, qx_s.at[d * 4], qx_r.at[d * 4], at_x(d))
    for e in (1, 3, 2):
        block = dqg.at[x, lax.rem(zl + 4 - e, 4)]
        receive(block, qz_r.at[e], qz_s.at[e])
        for d in (1, 3):
            send(block, block, qx_s.at[d * 4 + e], qx_r.at[d * 4 + e], at_x(d))

    def relay(e):
        for part, d in enumerate((1, 3)):
            block = dqg.at[lax.rem(x + 4 - d, 4), lax.rem(zl + 4 - e, 4)]
            receive(block, qx_r.at[d * 4 + e], qx_s.at[d * 4 + e])
            block = block.at[:, pl.ds(part * 256, 256)]
            send(block, block, q2_s.at[part * 4 + e], q2_r.at[part * 4 + e], at_x(d))

    relay(0)

    for part in range(2):
        for e in RUN:
            rows = ROWS[part]
            receive(zr.at[e, rows], dz_r.at[e * 2 + part], dz_s.at[e * 2 + part])
    summed = t2[zl, h].astype(F32)
    for e in range(1, 8):
        summed = summed + zr[e].astype(F32)
    gk[x, zl] = summed.astype(BF)
    block = gk.at[x, zl]
    for d in (2, 1, 3):
        send(block, block, pz_s.at[d], pz_r.at[d], at_zl(d))
    for d in (2, 1, 3):
        send(block, block, px_s.at[d * 4], px_r.at[d * 4], at_x(d))
    for e in (1, 3, 2):
        relay(e)
    for e in (1, 3, 2):
        block = gk.at[x, lax.rem(zl + 4 - e, 4)]
        receive(block, pz_r.at[e], pz_s.at[e])
        for d in (2, 1, 3):
            send(block, block, px_s.at[d * 4 + e], px_r.at[d * 4 + e], at_x(d))
    for d in (1, 3, 2):
        there = lax.rem(y + 4 - d, 4)
        block = xg.at[there, :, k]
        receive(block, xy_r.at[d], xy_s.at[d])
        send(block, block, xc_s.at[d], xc_r.at[d], mate)

    receive(wqt.at[pl.ds(pl.multiple_of((1 - k) * 256, 256), 256)], w_r.at[0], w_s.at[0])
    receive(wkv.at[pl.ds(pl.multiple_of((1 - k) * 64, 64), 64)], w_r.at[1], w_s.at[1])
    for e in range(4):
        for part in range(2):
            block = dqg.at[lax.rem(x + 2, 4), lax.rem(zl + 4 - e, 4), :, pl.ds(part * 256, 256)]
            receive(block, q2_r.at[part * 4 + e], q2_s.at[part * 4 + e])
    for d in (1, 3, 2):
        there = lax.rem(x + 4 - d, 4)
        for e in range(4):
            block = gk.at[there, lax.rem(zl + 4 - e, 4)]
            receive(block, px_r.at[d * 4 + e], px_s.at[d * 4 + e])

    def input_part(c):
        rows = slice(c * 16, (c + 1) * 16)
        gi[c] = (
            (
                dot(dqg[:, :, rows, :].reshape(256, 512), wqt[...])
                + dot(gk[:, :, rows, :].reshape(256, 128), wkv[...])
            )
            .astype(BF)
            .reshape(4, 4, 16, 512)
        )

    def input_send(c):
        return [
            send(
                gi.at[c, lax.rem(y + d, 4)], gyr.at[c, d],
                gy_s.at[c * 4 + d], gy_r.at[c * 4 + d], at_y(d),
            )
            for d in (2, 1, 3)
        ]

    def sent(copies):
        for copy in copies:
            copy.wait_send()
            pending[:] = [other for other in pending if other is not copy]

    def input_sum(c):
        for d in (1, 3, 2):
            receive(gyr.at[c, d], gy_r.at[c * 4 + d], gy_s.at[c * 4 + d])
        gys[c] = (
            gi[c, y].astype(F32)
            + gyr[c, 1].astype(F32)
            + gyr[c, 2].astype(F32)
            + gyr[c, 3].astype(F32)
        ).astype(BF)
        for d in (2, 1, 3):
            send(
                gys.at[c, lax.rem(zh + d, 4)], gzr.at[c, d],
                gz_s.at[c * 4 + d], gz_r.at[c * 4 + d], at_zh(d),
            )

    for there in range(4):
        send(dqg.at[there, :, :, other], dqm.at[there], qc_s.at[there], qc_r.at[there], mate)
        send(gk.at[there], gkm.at[there], pc_s.at[there], pc_r.at[there], mate)
    flying = []
    for c in range(5):
        input_part(c)
        if c == 4:
            input_sum(0)
        if c >= 2:
            sent(flying[c - 2])
        flying.append(input_send(c))

    input_sum(1)
    for there in range(4):
        receive(dqm.at[there], qc_r.at[there], qc_s.at[there])
        receive(gkm.at[there], pc_r.at[there], pc_s.at[there])
    for d in (0, 1, 3, 2):
        there = lax.rem(y + 4 - d, 4)
        receive(xg.at[there, :, 1 - k], xc_r.at[d], xc_s.at[d])
    accq[...] = jnp.zeros_like(accq)
    acck[...] = jnp.zeros_like(acck)

    def weight_step(b, _):
        here = xg[b, :, k].reshape(4 * HALF, 512)
        accq[...] += dot_first(here, dqg[b, :, :, mine].reshape(4 * HALF, 256))
        acck[...] += dot_first(gk[b].reshape(4 * HALF, 128), here)
        here = xg[b, :, 1 - k].reshape(4 * HALF, 512)
        accq[...] += dot_first(here, dqm[b].reshape(4 * HALF, 256))
        acck[...] += dot_first(gkm[b].reshape(4 * HALF, 128), here)
        return 0

    def weight_part(first, last):
        lax.fori_loop(first, last, weight_step, 0)

    weight_part(0, 1)
    for c in range(2, 5):
        input_sum(c)
        weight_part(c - 1, c)
    gwq_ref[...] = accq[...]
    gwk_ref[...] = acck[pl.ds(pl.multiple_of(k * 64, 64), 32), :]
    gwv_ref[...] = acck[pl.ds(pl.multiple_of(k * 64 + 32, 32), 32), :]
    for c in range(5):
        for d in (1, 3, 2):
            receive(gzr.at[c, d], gz_r.at[c * 4 + d], gz_s.at[c * 4 + d])
        gi_ref[c * 16 : (c + 1) * 16, :] = (
            gys[c, zh].astype(F32)
            + gzr[c, 1].astype(F32)
            + gzr[c, 2].astype(F32)
            + gzr[c, 3].astype(F32)
        ).astype(BF)
    for copy in pending:
        copy.wait_send()


def write_out(a, b, c, d, a_out, b_out, c_out, d_out, a_tmp, b_tmp, c_tmp, d_tmp, sems):
    ins, temps, outs = (a, b, c, d), (a_tmp, b_tmp, c_tmp, d_tmp), (a_out, b_out, c_out, d_out)
    reads = [pltpu.make_async_copy(ins[i], temps[i], sems.at[0, i]) for i in range(4)]
    writes = [pltpu.make_async_copy(temps[i], outs[i], sems.at[1, i]) for i in range(4)]
    for read in reads:
        read.start()
    for read, write in zip(reads, writes):
        read.wait()
        write.start()
    for write in writes:
        write.wait()


def shards(
    layer_input, w_query, w_key, w_value, query, key, value, context_gradient, positions, segments
):
    vmem = pl.BlockSpec(memory_space=pltpu.VMEM)
    b = lambda *shape: pltpu.VMEM(shape, BF)
    f = lambda *shape: pltpu.VMEM(shape, F32)
    scratch = [
        b(512, 256), b(32, 512), b(32, 512), b(TOK, 256), b(32, TOK), b(32, TOK), b(TOK, 256),
        pltpu.VMEM((1, TOK), jnp.int32), pltpu.VMEM((1, TOK), jnp.int32),
        b(2, 4, 8, HALF, 128), b(4, 4, 16, 256), f(4, TOK, HEAD), f(4, TOK, HEAD), b(256, 256),
        b(16, TOK, 128), b(16, TOK, 128), f(16, TOK, LANES), f(16, TOK, LANES), b(16, TOK, LANES), b(16, TOK, LANES),
        b(128, LANES), b(128, LANES), b(LANES, 128), b(LANES, 128),
        b(512, 512), b(128, 512), f(128, LANES),
        b(2, 4, 4, 2, HALF, 128), b(4, 4, 2, HALF, 128), b(4, 4, 2, HALF, 128),
        b(4, 4, 2, HALF, 128), b(4, 2, HALF, 128), b(8, HALF, 128),
        b(4, 4, HALF, 128), b(4, 4, HALF, 128),
        b(2, HALF, 256), b(4, 4, HALF, 512), b(4, 4, HALF, 256), b(4, 4, 2, HALF, 512),
        b(5, 4, 4, 16, 512), b(5, 4, 4, 16, 512), b(5, 4, 16, 512), b(5, 4, 16, 512),
        f(512, 256), f(128, 512), pltpu.SemaphoreType.DMA((10,)),
    ]
    sizes = [4, 4, 8, 32, 4, 2, 4, 4, 4, 4, 8, 16, 4, 16, 4, 1, 4, 16, 8, 4, 20, 20]
    for size in sizes:
        scratch += [pltpu.SemaphoreType.DMA((size,)), pltpu.SemaphoreType.DMA((size,))]
    gi, gwq, gwk, gwv = pl.pallas_call(
        kernel,
        out_shape=(
            jax.ShapeDtypeStruct((HALF, 512), BF),
            jax.ShapeDtypeStruct((512, 256), F32),
            jax.ShapeDtypeStruct((32, 512), F32),
            jax.ShapeDtypeStruct((32, 512), F32),
        ),
        in_specs=[pl.BlockSpec(memory_space=pl.ANY)] * 10,
        out_specs=(vmem,) * 4,
        scratch_shapes=scratch,
        compiler_params=pltpu.CompilerParams(
            collective_id=0, has_side_effects=True, vmem_limit_bytes=VMEM_BYTES
        ),
        name="attention_backward",
    )(
        layer_input, w_query, w_key.T, w_value.T, query, key.T, value.T, context_gradient,
        positions.reshape(1, TOK), segments.reshape(1, TOK),
    )
    results = (gi, gwq, gwk, gwv)
    anywhere = pl.BlockSpec(memory_space=pl.ANY)
    gi, gwq, gwk, gwv = pl.pallas_call(
        write_out,
        out_shape=tuple(jax.ShapeDtypeStruct(r.shape, r.dtype) for r in results),
        in_specs=[anywhere] * 4,
        out_specs=(anywhere,) * 4,
        scratch_shapes=[pltpu.VMEM(r.shape, r.dtype) for r in results]
        + [pltpu.SemaphoreType.DMA((2, 4))],
        compiler_params=pltpu.CompilerParams(vmem_limit_bytes=VMEM_BYTES),
        name="write_out",
    )(*results)
    return gi, gwq, gwk.T, gwv.T


def solution(mesh):
    return jax.shard_map(
        shards,
        mesh=mesh,
        in_specs=(P("col", "row"),) + (P("row", "col"),) * 7 + (P("row"),) * 2,
        out_specs=(P("col", "row"), P("row", "col"), P("row", "col"), P("row", "col")),
        check_vma=False,
    )
```

```python
import math

import jax
import jax.numpy as jnp
from jax import lax
from jax.experimental import pallas as pl
from jax.experimental.pallas import tpu as pltpu
from jax.sharding import PartitionSpec as P

MESH = pl.DeviceIdType.MESH
BF = jnp.bfloat16
F32 = jnp.float32
HEAD = 128
TOK = 160
HALF = 80
LANES = 384
ROPE_BASE = 500000.0
VMEM_BYTES = 127 * 2**19
SCALE = HEAD ** (-0.5)
RUN = (4, 5, 3, 6, 2, 7, 1)
ROWS = (pl.ds(0, 48), pl.ds(48, 32))


def dot(a, b):
    return lax.dot_general(a, b, (((1,), (0,)), ((), ())), preferred_element_type=F32)


def dot_first(a, b):
    return lax.dot_general(a, b, (((0,), (0,)), ((), ())), preferred_element_type=F32)


def unrotate(gradient, cosines, sines):
    return gradient * cosines + pltpu.roll(gradient, HEAD // 2, 1) * sines


def kernel(
    x_hbm, wq_hbm, wk_hbm, wv_hbm, q_hbm, k_hbm, v_hbm, o_hbm, pos_hbm, seg_hbm,
    gi_ref, gwq_ref, gwk_ref, gwv_ref,
    wq_ref, wk_ref, wv_ref, q_ref, k_ref, v_ref, o_ref, pos_ref, seg_ref,
    kv, meta, cosine, sine, perm, kf, vf, sc, dw, ds, low, qt, ot, qr, orow, wqt, wkv, dqacc,
    dkp, dkr, t1, xr, t2, zr, gk, gkm, dqo, dqg, dqm, xg, gi, gyr, gys, gzr, accq, acck,
    load, mz_s, mz_r, mx_s, mx_r, kz_s, kz_r, kx_s, kx_r, kc_s, kc_r, w_s, w_r,
    xz_s, xz_r, xy_s, xy_r, xc_s, xc_r,
    dc_s, dc_r, dx_s, dx_r, dz_s, dz_r, pz_s, pz_r, px_s, px_r, pc_s, pc_r,
    qm_s, qm_r, qz_s, qz_r, qx_s, qx_r, q2_s, q2_r, qc_s, qc_r, gy_s, gy_r, gz_s, gz_r,
):
    row, col = lax.axis_index("row"), lax.axis_index("col")
    x, zl = lax.div(row, 4), lax.rem(row, 4)
    y, zh, k = lax.div(col, 8), lax.rem(lax.div(col, 2), 4), lax.rem(col, 2)
    pair, h = lax.div(zh, 2), lax.rem(zh, 2)
    w = h * 4 + zl

    def device(x_=x, zl_=zl, y_=y, zh_=zh, k_=k):
        return (x_ * 4 + zl_, y_ * 8 + zh_ * 2 + k_)

    def at_x(d):
        return device(x_=lax.rem(x + d, 4))

    def at_y(d):
        return device(y_=lax.rem(y + d, 4))

    def at_zh(d):
        return device(zh_=lax.rem(zh + d, 4))

    def at_zl(d):
        return device(zl_=lax.rem(zl + d, 4))

    def at_run(e):
        there = lax.rem(w + e, 8)
        return device(zl_=lax.rem(there, 4), zh_=pair * 2 + lax.div(there, 4))

    mate = device(k_=1 - k)
    across = device(zh_=pair * 2 + 1 - h)
    far = [device(zh_=(1 - pair) * 2 + i) for i in range(2)]

    pending = []

    def send(src, dst, s_sem, r_sem, to):
        copy = pltpu.make_async_remote_copy(
            src_ref=src, dst_ref=dst, send_sem=s_sem, recv_sem=r_sem,
            device_id=to, device_id_type=MESH,
        )
        copy.start()
        pending.append(copy)
        return copy

    def receive(dst, r_sem, s_sem):
        pltpu.make_async_remote_copy(
            src_ref=dst, dst_ref=dst, send_sem=s_sem, recv_sem=r_sem,
            device_id=mate, device_id_type=MESH,
        ).wait_recv()

    barrier = pltpu.get_barrier_semaphore()
    peers = [mate] + far
    peers += [at_x(d) for d in (1, 2, 3)] + [at_y(d) for d in (1, 2, 3)]
    peers += [at_run(e) for e in range(1, 8)]
    for peer in peers:
        pl.semaphore_signal(barrier, inc=1, device_id=peer, device_id_type=MESH)

    loads = [
        pltpu.make_async_copy(src, dst, load.at[i])
        for i, (src, dst) in enumerate([
            (k_hbm, k_ref), (v_hbm, v_ref), (pos_hbm, pos_ref), (seg_hbm, seg_ref),
            (x_hbm, xg.at[y, zh, k]), (wk_hbm, wk_ref), (wv_hbm, wv_ref), (wq_hbm, wq_ref),
            (q_hbm, q_ref), (o_hbm, o_ref),
        ])
    ]
    for copy in loads:
        copy.start()
    for copy in loads[:4]:
        copy.wait()

    both = jnp.concatenate([k_ref[...], v_ref[...]], axis=0).astype(F32).T
    kv[k, x, w] = jnp.concatenate([both[:HALF], both[HALF:]], axis=1).astype(BF)
    first_count = jnp.sum(jnp.where(seg_ref[...] == 0, 1.0, 0.0), axis=1, keepdims=True)
    high = lax.div(pos_ref[...], 64)
    rest = pos_ref[...] - high * 64
    line = lax.broadcasted_iota(jnp.int32, (16, TOK), 0)
    facts = jnp.where(line == 0, first_count, jnp.where(line == 1, high.astype(F32), rest.astype(F32)))
    meta[x, zl, :, 0:TOK] = facts.astype(BF)
    meta[x, zl, :, TOK:256] = jnp.zeros((16, 256 - TOK), BF)

    pl.semaphore_wait(barrier, len(peers))

    block = kv.at[k, x, w]
    for d in (2, 1, 3):
        send(block, block, kz_s.at[d], kz_r.at[d], at_zl(d))
    send(block, block, kz_s.at[4], kz_r.at[4], across)
    block = meta.at[x, zl]
    for d in (2, 1, 3):
        send(block, block, mz_s.at[d], mz_r.at[d], at_zl(d))
    block = kv.at[k, x, w]
    for d in (1, 3):
        send(block, block, kx_s.at[d * 8], kx_r.at[d * 8], at_x(d))

    for copy in loads[4:]:
        copy.wait()
    for i in range(2):
        qr[i * TOK : (i + 1) * TOK] = q_ref[:, i * 128 : (i + 1) * 128]
        orow[i * TOK : (i + 1) * TOK] = o_ref[:, i * 128 : (i + 1) * 128]
    qr[2 * TOK : LANES] = jnp.zeros((LANES - 2 * TOK, 128), BF)
    orow[2 * TOK : LANES] = jnp.zeros((LANES - 2 * TOK, 128), BF)
    qt[...] = qr[...].astype(F32).T.astype(BF)
    ot[...] = orow[...].astype(F32).T.astype(BF)

    def run_block(e):
        if e < 4:
            return kv.at[k, x, h * 4 + lax.rem(zl + 4 - e, 4)]
        return kv.at[k, x, (1 - h) * 4 + lax.rem(zl + 8 - e, 4)]

    for e in (1, 3, 2, 4):
        block = run_block(e)
        receive(block, kz_r.at[e], kz_s.at[e])
        if e == 4:
            for d in (2, 1, 3):
                send(block, block, kz_s.at[4 + d], kz_r.at[4 + d], at_zl(d))
        for d in (1, 3):
            send(block, block, kx_s.at[d * 8 + e], kx_r.at[d * 8 + e], at_x(d))
    for d in (1, 3, 2):
        receive(meta.at[x, lax.rem(zl + 4 - d, 4)], mz_r.at[d], mz_s.at[d])
    for d in (1, 3, 2):
        send(meta.at[x], meta.at[x], mx_s.at[d], mx_r.at[d], at_x(d))
    for e in (5, 7, 6):
        block = run_block(e)
        receive(block, kz_r.at[e], kz_s.at[e])
        for d in (1, 3):
            send(block, block, kx_s.at[d * 8 + e], kx_r.at[d * 8 + e], at_x(d))
    send(kv.at[k, x], kv.at[k, x], kx_s.at[16], kx_r.at[16], at_x(2))
    send(kv.at[k, x], kv.at[k, x], kc_s.at[0], kc_r.at[0], mate)
    block = xg.at[y, zh, k]
    for d in (2, 1, 3):
        send(block, block, xz_s.at[d], xz_r.at[d], at_zh(d))

    source = lax.broadcasted_iota(jnp.int32, (256, 256), 0)
    target = lax.broadcasted_iota(jnp.int32, (256, 256), 1)
    wanted = lax.rem(lax.div(target, 32), 2) * 128 + lax.div(target, 64) * 32 + lax.rem(target, 32)
    perm[...] = jnp.where(source == wanted, 1.0, 0.0).astype(BF)
    for d in (1, 3, 2):
        receive(meta.at[lax.rem(x + 4 - d, 4)], mx_r.at[d], mx_s.at[d])
    cut = jnp.zeros((1, 1), F32)
    for xx in range(4):
        for zz in range(4):
            cut = cut + meta[xx, zz].astype(F32)[0:1, 0:1]
    lane = lax.broadcasted_iota(jnp.int32, (1, LANES), 1)
    query = lane - TOK * (lane >= TOK).astype(jnp.int32) - TOK * (lane >= 2 * TOK).astype(jnp.int32)
    query = query + row * TOK
    cut = jnp.broadcast_to(cut, (1, LANES)).astype(jnp.int32)
    begin = jnp.where(query < cut, 0, cut)

    def products(there, peak):
        def step(i, peak):
            at = there * 4 + i
            for half in range(2):
                parts = [kv[kk, there, hh * 4 + i] for hh in range(2) for kk in range(2)]
                lo = 64 * half
                kf[at, half * HALF : (half + 1) * HALF, :] = jnp.concatenate(
                    [p[:, lo : lo + 32] for p in parts], axis=1
                )
                vf[at, half * HALF : (half + 1) * HALF, :] = jnp.concatenate(
                    [p[:, lo + 32 : lo + 64] for p in parts], axis=1
                )
            dw[at] = dot(vf[at], ot[...])
            key = at * TOK + lax.broadcasted_iota(jnp.int32, (TOK, LANES), 0)
            seen = (key >= begin) & (key <= query)
            seen = jnp.where(seen, dot(kf[at], qt[...]) * SCALE, -1e30)
            sc[at] = seen
            return jnp.maximum(peak, jnp.max(seen, axis=0, keepdims=True))

        return lax.fori_loop(0, 4, step, peak, unroll=2)

    receive(kv.at[1 - k, x], kc_r.at[0], kc_s.at[0])
    peak = products(x, jnp.full((1, LANES), -1e30, F32))
    def pass_on(d):
        there = lax.rem(x + 4 - d, 4)
        if d == 2:
            receive(kv.at[k, there], kx_r.at[16], kx_s.at[16])
        else:
            for e in range(8):
                near = h * 4 + lax.rem(zl + 4 - e, 4)
                at = near if e < 4 else (1 - h) * 4 + lax.rem(zl + 8 - e, 4)
                receive(kv.at[k, there, at], kx_r.at[d * 8 + e], kx_s.at[d * 8 + e])
        send(kv.at[k, there], kv.at[k, there], kc_s.at[d], kc_r.at[d], mate)

    pass_on(1)
    pass_on(3)
    place = lax.broadcasted_iota(jnp.int32, (HEAD // 2, TOK), 0).astype(F32)
    freq = jnp.exp(-(2.0 * place / HEAD) * math.log(ROPE_BASE))

    def tables(i, _):
        facts = meta[x, i].astype(F32)
        angle = (facts[1:2, 0:TOK] * 64.0 + facts[2:3, 0:TOK]) * freq
        cos, sin = jnp.cos(angle), jnp.sin(angle)
        cosine[i] = jnp.concatenate([cos, cos], axis=0).T
        sine[i] = jnp.concatenate([sin, -sin], axis=0).T
        return 0

    lax.fori_loop(0, 4, tables, 0)
    for d in (1, 3, 2):
        there = lax.rem(x + 4 - d, 4)
        receive(kv.at[1 - k, there], kc_r.at[d], kc_s.at[d])
        peak = products(there, peak)
        if d == 1:
            pass_on(2)


    def sum_step(b, sums):
        total, delta = sums
        term = jnp.exp(sc[b] - peak)
        sc[b] = term
        return (
            total + jnp.sum(term, axis=0, keepdims=True),
            delta + jnp.sum(term * dw[b], axis=0, keepdims=True),
        )

    zero = jnp.zeros((1, LANES), F32)
    total, delta = lax.fori_loop(0, 16, sum_step, (zero, zero))
    inverse = 1.0 / total
    delta = delta * inverse

    dqacc[...] = jnp.zeros_like(dqacc)
    cosines, sines = cosine[zl], sine[zl]

    def key_send(d, part):
        there, rows = lax.rem(x + d, 4), ROWS[part]
        send(
            t1.at[there, :, :, rows], xr.at[d, :, :, rows],
            dx_s.at[d * 2 + part], dx_r.at[d * 2 + part], at_x(d),
        )

    def key_sum(d):
        there = lax.rem(x + d, 4)
        receive(dkr.at[there], dc_r.at[d], dc_s.at[d])
        t1[there] = (dkp[k, there].astype(F32) + dkr[there].astype(F32)).astype(BF)
        if d:
            key_send(d, 0)

    def score_grads(there, _):
        for i in range(4):
            b = there * 4 + i
            weights = sc[b] * inverse
            ds[b] = (weights * (dw[b] - delta) * SCALE).astype(BF)
            low[b] = weights.astype(BF)
        dqacc[...] += dot_first(
            kf[pl.ds(there * 4, 4)].reshape(4 * TOK, HEAD),
            ds[pl.ds(there * 4, 4)].reshape(4 * TOK, LANES),
        )
        return 0

    before = None
    for d in (2, 1, 3, 0):
        there = lax.rem(x + d, 4)
        score_grads(there, 0)

        def grad_step(i, _):
            b = there * 4 + i
            dkey = dot(ds[b], qr[...]).astype(BF)
            dvalue = dot(low[b], orow[...]).astype(BF)
            for half in range(2):
                dkp[half, there, i, 0] = dkey[half * HALF : (half + 1) * HALF]
                dkp[half, there, i, 1] = dvalue[half * HALF : (half + 1) * HALF]
            return 0

        lax.fori_loop(0, 4, grad_step, 0, unroll=2)
        send(dkp.at[1 - k, there], dkr.at[there], dc_s.at[d], dc_r.at[d], mate)
        if before is not None:
            key_sum(before)
        before = d
    dquery = dqacc[...].T
    for head in range(2):
        part = dquery[head * TOK : (head + 1) * TOK]
        both = unrotate(part, cosines, sines).astype(BF)
        for half in range(2):
            dqo[half, :, head * 128 : (head + 1) * 128] = both[half * HALF : (half + 1) * HALF]
    mine = pl.ds(pl.multiple_of(k * 256, 256), 256)
    other = pl.ds(pl.multiple_of((1 - k) * 256, 256), 256)
    send(dqo.at[1 - k], dqg.at[x, zl, :, mine], qm_s.at[0], qm_r.at[0], mate)
    dqg[x, zl, :, mine] = dqo[k]

    key_sum(0)
    for d in (2, 1, 3):
        key_send(d, 1)
    receive(dqg.at[x, zl, :, other], qm_r.at[0], qm_s.at[0])
    block = dqg.at[x, zl]
    for e in (2, 1, 3):
        send(block, block, qz_s.at[e], qz_r.at[e], at_zl(e))

    rows = pl.ds(pl.multiple_of(k * 64, 64), 64)
    wkv[rows, :] = jnp.concatenate([wk_ref[...], wv_ref[...]], axis=0)
    send(wkv.at[rows], wkv.at[rows], w_s.at[1], w_r.at[1], mate)
    rows = pl.ds(pl.multiple_of(k * 256, 256), 256)
    wqt[rows, :] = wq_ref[...].astype(F32).T.astype(BF)
    send(wqt.at[rows], wqt.at[rows], w_s.at[0], w_r.at[0], mate)
    for d in (1, 3, 2):
        receive(xg.at[y, lax.rem(zh + 4 - d, 4), k], xz_r.at[d], xz_s.at[d])
    block = xg.at[y, :, k]
    for d in (2, 1, 3):
        send(block, block, xy_s.at[d], xy_r.at[d], at_y(d))
    send(block, block, xc_s.at[0], xc_r.at[0], mate)

    def x_sum(part):
        lo, size = (0, 48) if part == 0 else (48, 32)
        at = pl.ds(pl.multiple_of(k * HALF + lo, 16), size)

        def step(i, _):
            total = t1[x, i, :, lo : lo + size].astype(F32)
            for d in range(1, 4):
                total = total + xr[d, i, :, lo : lo + size].astype(F32)
            turned = unrotate(total[0], cosine[i, at, :], sine[i, at, :])
            wide = jnp.concatenate([turned, total[1]], axis=1).astype(BF)
            wide = dot(wide, perm[...]).astype(BF)
            t2[i, 0, lo : lo + size] = wide[:, :128]
            t2[i, 1, lo : lo + size] = wide[:, 128:]
            return 0

        lax.fori_loop(0, 4, step, 0, unroll=True)

    for part in range(2):
        for d in (1, 3, 2):
            rows = ROWS[part]
            receive(xr.at[d, :, :, rows], dx_r.at[d * 2 + part], dx_s.at[d * 2 + part])
        x_sum(part)
        for e in RUN:
            to = lax.rem(w + e, 8)
            send(
                t2.at[lax.rem(to, 4), lax.div(to, 4), rows], zr.at[e, rows],
                dz_s.at[e * 2 + part], dz_r.at[e * 2 + part], at_run(e),
            )

    block = dqg.at[x, zl]
    for d in (1, 3):
        send(block, block, qx_s.at[d * 4], qx_r.at[d * 4], at_x(d))
    for e in (1, 3, 2):
        block = dqg.at[x, lax.rem(zl + 4 - e, 4)]
        receive(block, qz_r.at[e], qz_s.at[e])
        for d in (1, 3):
            send(block, block, qx_s.at[d * 4 + e], qx_r.at[d * 4 + e], at_x(d))

    def relay(e):
        for part, d in enumerate((1, 3)):
            block = dqg.at[lax.rem(x + 4 - d, 4), lax.rem(zl + 4 - e, 4)]
            receive(block, qx_r.at[d * 4 + e], qx_s.at[d * 4 + e])
            block = block.at[:, pl.ds(part * 256, 256)]
            send(block, block, q2_s.at[part * 4 + e], q2_r.at[part * 4 + e], at_x(d))

    relay(0)

    for part in range(2):
        for e in RUN:
            rows = ROWS[part]
            receive(zr.at[e, rows], dz_r.at[e * 2 + part], dz_s.at[e * 2 + part])
    summed = t2[zl, h].astype(F32)
    for e in range(1, 8):
        summed = summed + zr[e].astype(F32)
    gk[x, zl] = summed.astype(BF)
    block = gk.at[x, zl]
    for d in (2, 1, 3):
        send(block, block, pz_s.at[d], pz_r.at[d], at_zl(d))
    for d in (2, 1, 3):
        send(block, block, px_s.at[d * 4], px_r.at[d * 4], at_x(d))
    for e in (1, 3, 2):
        relay(e)
    for e in (1, 3, 2):
        block = gk.at[x, lax.rem(zl + 4 - e, 4)]
        receive(block, pz_r.at[e], pz_s.at[e])
        for d in (2, 1, 3):
            send(block, block, px_s.at[d * 4 + e], px_r.at[d * 4 + e], at_x(d))
    for d in (1, 3, 2):
        there = lax.rem(y + 4 - d, 4)
        block = xg.at[there, :, k]
        receive(block, xy_r.at[d], xy_s.at[d])
        send(block, block, xc_s.at[d], xc_r.at[d], mate)

    receive(wqt.at[pl.ds(pl.multiple_of((1 - k) * 256, 256), 256)], w_r.at[0], w_s.at[0])
    receive(wkv.at[pl.ds(pl.multiple_of((1 - k) * 64, 64), 64)], w_r.at[1], w_s.at[1])
    for e in range(4):
        for part in range(2):
            block = dqg.at[lax.rem(x + 2, 4), lax.rem(zl + 4 - e, 4), :, pl.ds(part * 256, 256)]
            receive(block, q2_r.at[part * 4 + e], q2_s.at[part * 4 + e])
    for d in (1, 3, 2):
        there = lax.rem(x + 4 - d, 4)
        for e in range(4):
            block = gk.at[there, lax.rem(zl + 4 - e, 4)]
            receive(block, px_r.at[d * 4 + e], px_s.at[d * 4 + e])

    def input_part(c):
        rows = slice(c * 16, (c + 1) * 16)
        gi[c] = (
            (
                dot(dqg[:, :, rows, :].reshape(256, 512), wqt[...])
                + dot(gk[:, :, rows, :].reshape(256, 128), wkv[...])
            )
            .astype(BF)
            .reshape(4, 4, 16, 512)
        )

    def input_send(c):
        return [
            send(
                gi.at[c, lax.rem(y + d, 4)], gyr.at[c, d],
                gy_s.at[c * 4 + d], gy_r.at[c * 4 + d], at_y(d),
            )
            for d in (2, 1, 3)
        ]

    def sent(copies):
        for copy in copies:
            copy.wait_send()
            pending[:] = [other for other in pending if other is not copy]

    def input_sum(c):
        for d in (1, 3, 2):
            receive(gyr.at[c, d], gy_r.at[c * 4 + d], gy_s.at[c * 4 + d])
        gys[c] = (
            gi[c, y].astype(F32)
            + gyr[c, 1].astype(F32)
            + gyr[c, 2].astype(F32)
            + gyr[c, 3].astype(F32)
        ).astype(BF)
        for d in (2, 1, 3):
            send(
                gys.at[c, lax.rem(zh + d, 4)], gzr.at[c, d],
                gz_s.at[c * 4 + d], gz_r.at[c * 4 + d], at_zh(d),
            )

    for there in range(4):
        send(dqg.at[there, :, :, other], dqm.at[there], qc_s.at[there], qc_r.at[there], mate)
        send(gk.at[there], gkm.at[there], pc_s.at[there], pc_r.at[there], mate)
    flying = []
    for c in range(5):
        input_part(c)
        if c == 4:
            input_sum(0)
        if c >= 2:
            sent(flying[c - 2])
        flying.append(input_send(c))

    input_sum(1)
    for there in range(4):
        receive(dqm.at[there], qc_r.at[there], qc_s.at[there])
        receive(gkm.at[there], pc_r.at[there], pc_s.at[there])
    for d in (0, 1, 3, 2):
        there = lax.rem(y + 4 - d, 4)
        receive(xg.at[there, :, 1 - k], xc_r.at[d], xc_s.at[d])
    accq[...] = jnp.zeros_like(accq)
    acck[...] = jnp.zeros_like(acck)

    def weight_step(b, _):
        here = xg[b, :, k].reshape(4 * HALF, 512)
        accq[...] += dot_first(here, dqg[b, :, :, mine].reshape(4 * HALF, 256))
        acck[...] += dot_first(gk[b].reshape(4 * HALF, 128), here)
        here = xg[b, :, 1 - k].reshape(4 * HALF, 512)
        accq[...] += dot_first(here, dqm[b].reshape(4 * HALF, 256))
        acck[...] += dot_first(gkm[b].reshape(4 * HALF, 128), here)
        return 0

    def weight_part(first, last):
        lax.fori_loop(first, last, weight_step, 0)

    weight_part(0, 1)
    for c in range(2, 5):
        input_sum(c)
        weight_part(c - 1, c)
    gwq_ref[...] = accq[...]
    gwk_ref[...] = acck[pl.ds(pl.multiple_of(k * 64, 64), 32), :]
    gwv_ref[...] = acck[pl.ds(pl.multiple_of(k * 64 + 32, 32), 32), :]
    for c in range(5):
        for d in (1, 3, 2):
            receive(gzr.at[c, d], gz_r.at[c * 4 + d], gz_s.at[c * 4 + d])
        gi_ref[c * 16 : (c + 1) * 16, :] = (
            gys[c, zh].astype(F32)
            + gzr[c, 1].astype(F32)
            + gzr[c, 2].astype(F32)
            + gzr[c, 3].astype(F32)
        ).astype(BF)
    for copy in pending:
        copy.wait_send()


def write_out(a, b, c, d, a_out, b_out, c_out, d_out, a_tmp, b_tmp, c_tmp, d_tmp, sems):
    ins, temps, outs = (a, b, c, d), (a_tmp, b_tmp, c_tmp, d_tmp), (a_out, b_out, c_out, d_out)
    reads = [pltpu.make_async_copy(ins[i], temps[i], sems.at[0, i]) for i in range(4)]
    writes = [pltpu.make_async_copy(temps[i], outs[i], sems.at[1, i]) for i in range(4)]
    for read in reads:
        read.start()
    for read, write in zip(reads, writes):
        read.wait()
        write.start()
    for write in writes:
        write.wait()


def shards(
    layer_input, w_query, w_key, w_value, query, key, value, context_gradient, positions, segments
):
    vmem = pl.BlockSpec(memory_space=pltpu.VMEM)
    b = lambda *shape: pltpu.VMEM(shape, BF)
    f = lambda *shape: pltpu.VMEM(shape, F32)
    scratch = [
        b(512, 256), b(32, 512), b(32, 512), b(TOK, 256), b(32, TOK), b(32, TOK), b(TOK, 256),
        pltpu.VMEM((1, TOK), jnp.int32), pltpu.VMEM((1, TOK), jnp.int32),
        b(2, 4, 8, HALF, 128), b(4, 4, 16, 256), f(4, TOK, HEAD), f(4, TOK, HEAD), b(256, 256),
        b(16, TOK, 128), b(16, TOK, 128), f(16, TOK, LANES), f(16, TOK, LANES), b(16, TOK, LANES), b(16, TOK, LANES),
        b(128, LANES), b(128, LANES), b(LANES, 128), b(LANES, 128),
        b(512, 512), b(128, 512), f(128, LANES),
        b(2, 4, 4, 2, HALF, 128), b(4, 4, 2, HALF, 128), b(4, 4, 2, HALF, 128),
        b(4, 4, 2, HALF, 128), b(4, 2, HALF, 128), b(8, HALF, 128),
        b(4, 4, HALF, 128), b(4, 4, HALF, 128),
        b(2, HALF, 256), b(4, 4, HALF, 512), b(4, 4, HALF, 256), b(4, 4, 2, HALF, 512),
        b(5, 4, 4, 16, 512), b(5, 4, 4, 16, 512), b(5, 4, 16, 512), b(5, 4, 16, 512),
        f(512, 256), f(128, 512), pltpu.SemaphoreType.DMA((10,)),
    ]
    sizes = [4, 4, 8, 32, 4, 2, 4, 4, 4, 4, 8, 16, 4, 16, 4, 1, 4, 16, 8, 4, 20, 20]
    for size in sizes:
        scratch += [pltpu.SemaphoreType.DMA((size,)), pltpu.SemaphoreType.DMA((size,))]
    gi, gwq, gwk, gwv = pl.pallas_call(
        kernel,
        out_shape=(
            jax.ShapeDtypeStruct((HALF, 512), BF),
            jax.ShapeDtypeStruct((512, 256), F32),
            jax.ShapeDtypeStruct((32, 512), F32),
            jax.ShapeDtypeStruct((32, 512), F32),
        ),
        in_specs=[pl.BlockSpec(memory_space=pl.ANY)] * 10,
        out_specs=(vmem,) * 4,
        scratch_shapes=scratch,
        compiler_params=pltpu.CompilerParams(
            collective_id=0, has_side_effects=True, vmem_limit_bytes=VMEM_BYTES
        ),
        name="attention_backward",
    )(
        layer_input, w_query, w_key.T, w_value.T, query, key.T, value.T, context_gradient,
        positions.reshape(1, TOK), segments.reshape(1, TOK),
    )
    results = (gi, gwq, gwk, gwv)
    anywhere = pl.BlockSpec(memory_space=pl.ANY)
    gi, gwq, gwk, gwv = pl.pallas_call(
        write_out,
        out_shape=tuple(jax.ShapeDtypeStruct(r.shape, r.dtype) for r in results),
        in_specs=[anywhere] * 4,
        out_specs=(anywhere,) * 4,
        scratch_shapes=[pltpu.VMEM(r.shape, r.dtype) for r in results]
        + [pltpu.SemaphoreType.DMA((2, 4))],
        compiler_params=pltpu.CompilerParams(vmem_limit_bytes=VMEM_BYTES),
        name="write_out",
    )(*results)
    return gi, gwq, gwk.T, gwv.T


def solution(mesh):
    return jax.shard_map(
        shards,
        mesh=mesh,
        in_specs=(P("col", "row"),) + (P("row", "col"),) * 7 + (P("row"),) * 2,
        out_specs=(P("col", "row"), P("row", "col"), P("row", "col"), P("row", "col")),
        check_vma=False,
    )
```
